256 devices in a mesh: ctx: 64 (over z, y_lo, x), tp: 4 (over y_hi, core).
Axes of the slice: x: 4, y: 4 (y_hi: 2, y_lo: 2; y = y_hi * 2 + y_lo), z: 8, core: 2. Of those that a mesh axis runs over, the one named last changes fastest.
Arguments:
- prefill_queries: bfloat16 [12288, 5120], P('ctx', 'tp'), may hold values from -20 to 20
- prefill_keys: bfloat16 [12288, 1024], P('ctx', 'tp'), may hold values from -5 to 5
- prefill_values: bfloat16 [12288, 1024], P('ctx', 'tp'), may hold values from -6 to 6
- segments: int32 [12288], replicated, may hold values from 0 to 7, never falling along the last dimension, each value on 1 to 9216 neighbouring positions
- decode_queries: bfloat16 [3, 64, 5120], P(None, None, 'tp'), may hold values from -152 to 152
- decode_keys: bfloat16 [3, 64, 1024], P(None, 'ctx', 'tp'), may hold values from -12 to 12
- decode_values: bfloat16 [3, 64, 1024], P(None, 'ctx', 'tp'), may hold values from -4 to 4
- row_request: int32 [64], replicated, may hold values from 0 to 7
- norm_gain: float32 [5120], P('tp'), may hold values from 0.25 to 1.75
- head_weight: bfloat16 [5120, 98304], P('tp', 'ctx'), may hold values from -0.27155765 to 0.27155765
- allowed_tiles: int32 [3, 64, 32], replicated, may hold values from 0 to 767, as said below
- tokens: int32 [3, 64], replicated, may hold values from 0 to 98303, as said below
Outputs:
- prefill_output: bfloat16 [12288, 5120], P('ctx', 'tp')
- target_logprob: float32 [3, 64], P(None, 'ctx')
The draws below stay inside these ranges and needn't reach their ends.
Inputs may be any that keep to these rules, and one draw needn't show every extreme that they name: `segments`: positions are grouped by request in order, each request's prompt spans 1 to 9216 positions and one spans exactly 9216. `allowed_tiles`: the 32 tiles of a row are distinct; tile k holds ids k * 128 to k * 128 + 127. `tokens`: each token lies in one of the allowed tiles of its row and step.
All inputs are finite; a program needn't handle non-finite values.
Results may differ from the reference program's by a relative error of at most 0.011.
Values may be sent and summed in bfloat16 or wider, within the bound.
No kernel may reach another device: no remote copies, remote signals or barrier semaphores. Data moves between devices by JAX's collectives and lax.ppermute only.
A program may use at most 192 MiB of HBM per device.

```python
import math
import jax
import jax.numpy as jnp
import numpy as np
from jax import lax

D = 5120
QH = 40
KVH = 8
HD = 128
VOCAB = 98304
TILE = 128
TOK_DEV = 192
L = 12288
MOST = 9216
REQ = 8
ROWS = 64
STEPS = 3
ALLOW = 32
N_CTX = 64


def decode_base(key):
    return jnp.clip(jax.random.normal(jax.random.fold_in(key, 201), (ROWS, D), jnp.float32), -4.0, 4.0)


def first_tiles(row_key):
    return jax.random.permutation(row_key, VOCAB // TILE)[:ALLOW]


def tile_choice(key):
    row_keys = jax.random.split(jax.random.fold_in(key, 301), STEPS * ROWS)
    tile_lists = jax.vmap(first_tiles)(row_keys).reshape(STEPS, ROWS, ALLOW).astype(jnp.int32)
    pick_slot = jax.random.randint(jax.random.fold_in(key, 302), (STEPS, ROWS, 1), 0, ALLOW)
    offset = jax.random.randint(jax.random.fold_in(key, 303), (STEPS, ROWS), 0, TILE)
    picked = jnp.take_along_axis(tile_lists, pick_slot, axis=2)[..., 0]
    return (tile_lists, (picked * TILE + offset).astype(jnp.int32))


def draw_prefill_queries(key, part):
    key = jax.random.fold_in(key, 1)
    values = jnp.clip(jax.random.normal(key, (L, D), jnp.float32), -5.0, 5.0)
    return values.astype(jnp.bfloat16)


def draw_prefill_keys(key, part):
    key = jax.random.fold_in(key, 2)
    values = jnp.clip(jax.random.normal(key, (L, KVH * HD), jnp.float32), -5.0, 5.0)
    return values.astype(jnp.bfloat16)


def draw_decode_queries(key, part):
    base_rows = decode_base(key)
    key = jax.random.fold_in(key, 3)
    noise_draw = jnp.clip(jax.random.normal(key, (STEPS, ROWS, D), jnp.float32), -4.0, 4.0)
    values = base_rows[None] + 0.5 * noise_draw
    return values.astype(jnp.bfloat16)


def draw_decode_keys(key, part):
    base_rows = decode_base(key)
    key = jax.random.fold_in(key, 4)
    group_mean = base_rows.reshape(ROWS, KVH, QH // KVH, HD).mean(axis=2).reshape(ROWS, KVH * HD)
    noise_draw = jnp.clip(jax.random.normal(key, (STEPS, ROWS, KVH * HD), jnp.float32), -4.0, 4.0)
    values = 2.5 * group_mean[None] + 0.5 * noise_draw
    return values.astype(jnp.bfloat16)


def draw_decode_values(key, part):
    key = jax.random.fold_in(key, 7)
    noise_draw = jnp.clip(jax.random.normal(key, (STEPS, ROWS, KVH * HD), jnp.float32), -4.0, 4.0)
    values = noise_draw
    return values.astype(jnp.bfloat16)


def draw_head_weight(key, part):
    key = jax.random.fold_in(key, 8)
    base_draw = 3.0 / D ** 0.5 * jnp.clip(jax.random.normal(key, (D, VOCAB), jnp.float32), -6.0, 6.0)
    values = base_draw
    return values.astype(jnp.bfloat16)


def draw_allowed_tiles(key, part):
    tile_lists, picked = tile_choice(key)
    return tile_lists


def draw_tokens(key, part):
    tile_lists, picked = tile_choice(key)
    return picked


def touch_ends(result, own_key, least, top_value):
    dims = result.shape
    place = [jax.random.randint(jax.random.fold_in(own_key, axis), (), 0, dims[axis]) for axis in range(len(dims))]
    result = result.at[tuple(place)].set(least)
    longest = dims.index(max(dims))
    place[longest] = (place[longest] + 1) % dims[longest]
    return result.at[tuple(place)].set(top_value)


def block_levels(own_key, dims, cuts, smallest, top_value):
    def one(axis_at, shards_of):
        draws = jax.random.uniform(jax.random.fold_in(jax.random.fold_in(own_key, 6), axis_at), (shards_of,), jnp.float32, smallest / len(cuts), top_value / len(cuts))
        return jnp.repeat(jnp.exp(draws), dims[axis_at] // shards_of).reshape((-1,) + (1,) * (len(dims) - axis_at - 1))

    factor_of = one(*cuts[0])
    for cut in cuts[1:]:
        factor_of = factor_of * one(*cut)
    return factor_of


def split_up(count, total, reach, skew):
    portions = [(1 << 20) // math.isqrt(standing ** skew) + 1 for standing in range(2, count + 1)]
    surplus, holding = total - reach - (count - 1), [1] * (count - 1)
    while surplus > 0:
        movable = [i for i in range(count - 1) if holding[i] < reach]
        mass, left = sum([portions[i] for i in movable]), surplus
        for i in movable:
            addition = min(reach - holding[i], max(1, left * portions[i] // mass), surplus)
            holding[i] = holding[i] + addition
            surplus = surplus - addition
    return np.array([reach] + holding)


def ragged_sizes(rng, count, total, limit, slope):
    if count == 2:
        one = jax.random.randint(rng, (), max(1, total - limit), min(limit, total - 1) + 1)
        return jnp.stack([one, total - one])
    tallies = jnp.asarray(split_up(count, total, limit, slope), jnp.int32)
    couples = (count - 1) // 2
    donor, taker = tallies[1:1 + 2 * couples:2], tallies[2:2 + 2 * couples:2]
    margin = jnp.minimum(donor - 1, limit - taker)
    moved = jax.random.randint(jax.random.fold_in(rng, 1), (couples,), 0, 1 << 20) % (margin + 1)
    tallies = tallies.at[1:1 + 2 * couples:2].set(donor - moved).at[2:2 + 2 * couples:2].set(taker + moved)
    return tallies[jax.random.permutation(jax.random.fold_in(rng, 2), count)]


def gaussian(stream_key, extent, spread, reach, cuts=(), kind=jnp.bfloat16):
    level = block_levels(stream_key, extent, cuts, -0.22, 0.18) if cuts else 1.0
    drawn = jax.random.normal(stream_key, extent, jnp.float32) * spread * level
    return jnp.minimum(jnp.maximum(drawn, -reach), reach).astype(kind)


def setup_inputs(seed: int = 0) -> dict:
    streams_of = jax.random.split(jax.random.key(seed), 13)
    return {
        "prefill_queries": draw_prefill_queries(jax.random.fold_in(streams_of[12], 71), 0),
        "prefill_keys": draw_prefill_keys(jax.random.fold_in(streams_of[12], 71), 0),
        "prefill_values": gaussian(streams_of[2], (L, KVH * HD), 1.0, 6.0, ((0, 64), (1, 4))),
        "segments": jnp.searchsorted(jnp.cumsum(ragged_sizes(streams_of[3], REQ, L, MOST, 2)), jnp.arange(L), side="right").astype(jnp.int32),
        "decode_queries": draw_decode_queries(jax.random.fold_in(streams_of[12], 71), 0),
        "decode_keys": draw_decode_keys(jax.random.fold_in(streams_of[12], 71), 0),
        "decode_values": draw_decode_values(jax.random.fold_in(streams_of[12], 71), 0),
        "row_request": touch_ends(jax.random.randint(streams_of[7], (ROWS,), 0, REQ), jax.random.fold_in(streams_of[7], 1), 0, REQ - 1).astype(jnp.int32),
        "norm_gain": jnp.clip(1.0 + 0.15 * jax.random.normal(streams_of[8], (D,), jnp.float32), 0.25, 1.75),
        "head_weight": draw_head_weight(jax.random.fold_in(streams_of[12], 71), 0),
        "allowed_tiles": draw_allowed_tiles(jax.random.fold_in(streams_of[12], 71), 0),
        "tokens": draw_tokens(jax.random.fold_in(streams_of[12], 71), 0),
    }


epsilon = 1e-06
floor_value = -1e+30

def prefill_rows(first_row, prefill_queries, key_table, value_table, segments):
    group_size = QH // KVH
    row_count = TOK_DEV
    block = lax.dynamic_slice_in_dim(prefill_queries, first_row, row_count, 0)
    block = block.astype(jnp.float32).reshape(row_count, KVH, group_size, HD)
    places = jnp.arange(key_table.shape[0], dtype=jnp.int32)
    query_places = first_row + jnp.arange(row_count, dtype=jnp.int32)
    query_segment = lax.dynamic_slice_in_dim(segments, first_row, row_count, 0)
    admitted = (places[None, :] <= query_places[:, None]) & (segments[None, :] == query_segment[:, None])
    admitted = admitted[:, None, None, :]
    scores = jnp.einsum('qhgd,khd->qhgk', block, key_table) * HD ** (-0.5)
    masked = jnp.where(admitted, scores, floor_value)
    row_peak = lax.optimization_barrier(jnp.max(masked, axis=-1, keepdims=True))
    weights = jnp.where(admitted, jnp.exp(masked - row_peak), 0.0)
    row_total = lax.optimization_barrier(jnp.sum(weights, axis=-1))
    rounded = lax.optimization_barrier(weights.astype(jnp.bfloat16)).astype(jnp.float32)
    output = jnp.einsum('qhgk,khd->qhgd', rounded, value_table) / row_total[..., None]
    return output.reshape(row_count, QH * HD).astype(jnp.bfloat16)

def decode_attention(decode_queries, decode_keys, decode_values, row_request, key_table, value_table, segments):
    group_size = QH // KVH
    own_keys = decode_keys.astype(jnp.float32).reshape(STEPS, ROWS, KVH, HD)
    own_values = decode_values.astype(jnp.float32).reshape(STEPS, ROWS, KVH, HD)
    prompt_mask = (segments[None, :] == row_request[:, None])[:, None, None, :]
    step_order = jnp.arange(STEPS, dtype=jnp.int32)
    outputs = []
    for step_index in range(STEPS):
        queries = decode_queries[step_index].astype(jnp.float32).reshape(ROWS, KVH, group_size, HD)
        far_scores = jnp.einsum('rhgd,khd->rhgk', queries, key_table) * HD ** (-0.5)
        own_scores = jnp.einsum('rhgd,jrhd->rhgj', queries, own_keys) * HD ** (-0.5)
        own_mask = step_order <= step_index
        far_masked = jnp.where(prompt_mask, far_scores, floor_value)
        own_masked = jnp.where(own_mask, own_scores, floor_value)
        row_peak = jnp.maximum(lax.optimization_barrier(jnp.max(far_masked, axis=-1)), lax.optimization_barrier(jnp.max(own_masked, axis=-1)))[..., None]
        far_weights = jnp.where(prompt_mask, jnp.exp(far_masked - row_peak), 0.0)
        own_weights = jnp.where(own_mask, jnp.exp(own_masked - row_peak), 0.0)
        row_total = lax.optimization_barrier(jnp.sum(far_weights, axis=-1)) + lax.optimization_barrier(jnp.sum(own_weights, axis=-1))
        far_rounded = lax.optimization_barrier(far_weights.astype(jnp.bfloat16)).astype(jnp.float32)
        own_rounded = lax.optimization_barrier(own_weights.astype(jnp.bfloat16)).astype(jnp.float32)
        output = jnp.einsum('rhgk,khd->rhgd', far_rounded, value_table)
        output = output + jnp.einsum('rhgj,jrhd->rhgd', own_rounded, own_values)
        output = output / row_total[..., None]
        outputs.append(output.reshape(ROWS, QH * HD).astype(jnp.bfloat16))
    return jnp.stack(outputs)

def score_tokens(attention, norm_gain, head_weight, allowed_tiles, tokens):
    widened = attention.astype(jnp.float32)
    squares = lax.optimization_barrier(jnp.sum(widened * widened, axis=-1))
    row_scale = lax.rsqrt(squares / D + epsilon)
    scaled = (widened * norm_gain).astype(jnp.bfloat16)
    partial_value = jnp.dot(scaled.reshape(STEPS * ROWS, D), head_weight, preferred_element_type=jnp.float32)
    logits = row_scale[..., None] * partial_value.reshape(STEPS, ROWS, VOCAB)
    tile_ids = jnp.arange(VOCAB // TILE, dtype=jnp.int32)
    allowed = jnp.any(allowed_tiles[..., None] == tile_ids, axis=2)[..., None]
    blocks = logits.reshape(STEPS, ROWS, VOCAB // TILE, TILE)
    masked = jnp.where(allowed, blocks, floor_value)
    row_peak = lax.optimization_barrier(jnp.max(masked, axis=(2, 3)))
    exp_mass = lax.optimization_barrier(jnp.sum(jnp.where(allowed, jnp.exp(masked - row_peak[..., None, None]), 0.0), axis=(2, 3)))
    target = jnp.take_along_axis(logits, tokens[..., None].astype(jnp.int32), axis=2)[..., 0]
    return target - (row_peak + jnp.log(exp_mass))

def reference(prefill_queries, prefill_keys, prefill_values, segments, decode_queries, decode_keys, decode_values, row_request, norm_gain, head_weight, allowed_tiles, tokens):
    key_table = prefill_keys.astype(jnp.float32).reshape(-1, KVH, HD)
    value_table = prefill_values.astype(jnp.float32).reshape(-1, KVH, HD)
    starts = jnp.arange(N_CTX, dtype=jnp.int32) * TOK_DEV

    def one_block(first_row):
        return prefill_rows(first_row, prefill_queries, key_table, value_table, segments)
    prefill_output = lax.map(one_block, starts).reshape(N_CTX * TOK_DEV, QH * HD)
    attention = decode_attention(decode_queries, decode_keys, decode_values, row_request, key_table, value_table, segments)
    target_logprob = score_tokens(attention, norm_gain, head_weight, allowed_tiles, tokens)
    return (prefill_output, target_logprob)
```

```python
import functools
import math

import jax
import jax.numpy as jnp
from jax import lax
from jax.experimental import pallas as pl
from jax.experimental.pallas import tpu as pltpu
from jax.sharding import Mesh, PartitionSpec as P

HD = 128
TILE = 128
EPS = 1e-06
FLOOR = -1e30
BELOW = -2e30
LOG2E = 1.4426950408889634
BF = jnp.bfloat16
F32 = jnp.float32
CTX = ("z", "yl", "x")
TP = ("yh", "core")
KT = 512


def dot_t(a, b):
    return lax.dot_general(a, b, (((1,), (1,)), ((), ())), preferred_element_type=F32)


def dot(a, b):
    return lax.dot_general(a, b, (((1,), (0,)), ((), ())), preferred_element_type=F32)


def two_parts(value):
    high = value.astype(BF)
    return high, (value - high.astype(F32)).astype(BF)


def attend_kernel(
    shape, info, q_ref, start_ref, place_ref, kv_hbm, out_ref, keys, vals, qs, peak, acc, sem
):
    nz, ny, nx, rows, group = shape
    copies = []
    for z in range(nz):
        for x in range(nx):
            for y in range(ny):
                there = pl.ds(((z * ny + y) * nx + x) * rows, rows)
                k, v = kv_hbm.at[z * nx + x, 0, y], kv_hbm.at[z * nx + x, 1, y]
                copies.append(pltpu.make_async_copy(k, keys.at[there, 0:HD], sem))
                copies.append(pltpu.make_async_copy(k, keys.at[there, HD : 2 * HD], sem))
                copies.append(pltpu.make_async_copy(v, vals.at[there, 0:HD], sem))
    for copy in copies:
        copy.start()
    scale = HD**-0.5 * LOG2E
    for tile in range(ny):
        for h in range(group):
            q = q_ref[tile, :, h * HD : (h + 1) * HD].astype(F32) * scale
            high, low = two_parts(q)
            qs[tile, h, :, 0:HD] = high
            qs[tile, h, :, HD : 2 * HD] = low
    vals[:, HD : 2 * HD] = jnp.ones((vals.shape[0], HD), BF)
    for copy in copies:
        copy.wait()
    for tile in range(ny):
        first, last, inner_first, inner_last = (info[tile, i] for i in range(4))
        peak[...] = jnp.full(peak.shape, FLOOR, F32)
        acc[...] = jnp.zeros(acc.shape, F32)

        def step(turn, masked):
            base = pl.multiple_of(turn * KT, KT)
            k = keys[pl.ds(base, KT), :]
            v = vals[pl.ds(base, KT), :]
            if masked:
                at = base + lax.broadcasted_iota(jnp.int32, (rows, KT), 1)
                keep = (at >= start_ref[tile]) & (at <= place_ref[tile])
            for h in range(group):
                s = dot_t(qs[tile, h], k)
                if masked:
                    s = jnp.where(keep, s, BELOW)
                old = peak[h]
                new = jnp.maximum(old, jnp.max(s, axis=1, keepdims=True))
                peak[h] = new
                p = jnp.exp2(s - new).astype(BF)
                acc[h] = acc[h] * jnp.exp2(old - new) + dot(p, v)

        def turn_of(turn, _):
            inside = (turn >= inner_first) & (turn < inner_last)

            @pl.when(inside)
            def _():
                step(turn, False)

            @pl.when(jnp.logical_not(inside))
            def _():
                step(turn, True)

            return 0

        lax.fori_loop(first, last, turn_of, 0)
        for h in range(group):
            out_ref[tile, :, h * HD : (h + 1) * HD] = (acc[h, :, 0:HD] / acc[h, :, HD : 2 * HD]).astype(BF)


def attend(sizes, info, q, start, place, kv):
    nz, ny, nx = sizes
    rows, width = q.shape[1], q.shape[2]
    group = width // HD
    total = nz * ny * nx * rows
    vmem = pl.BlockSpec(memory_space=pltpu.VMEM)
    hbm = pl.BlockSpec(memory_space=pl.ANY)
    return pl.pallas_call(
        functools.partial(attend_kernel, (nz, ny, nx, rows, group)),
        out_shape=jax.ShapeDtypeStruct(q.shape, BF),
        in_specs=[pl.BlockSpec(memory_space=pltpu.SMEM), vmem, vmem, vmem, hbm],
        out_specs=vmem,
        scratch_shapes=[
            pltpu.VMEM((total, 2 * HD), BF),
            pltpu.VMEM((total, 2 * HD), BF),
            pltpu.VMEM((ny, group, rows, 2 * HD), BF),
            pltpu.VMEM((group, rows, 1), F32),
            pltpu.VMEM((group, rows, 2 * HD), F32),
            pltpu.SemaphoreType.DMA,
        ],
        compiler_params=pltpu.CompilerParams(vmem_limit_bytes=40 * 2**20),
        cost_estimate=pl.CostEstimate(
            flops=20_000_000_000, bytes_accessed=8_000_000, transcendentals=17_000_000
        ),
    )(info, q, start, place, kv)


def state_kernel(shape, q_ref, k_ref, v_ref, ok_ref, ov_ref, keep_ref, out_ref):
    steps, lines, kv_heads, group = shape
    rows, own = k_ref.shape[0], ok_ref.shape[0]
    count = keep_ref.shape[1]
    scale = HD**-0.5 * LOG2E
    keep = keep_ref[...] > 0
    lane = lax.broadcasted_iota(jnp.int32, (steps * lines, HD), 1)
    tail = jnp.zeros((steps * lines, HD), F32)
    for kh in range(kv_heads):
        at = slice(kh * HD, (kh + 1) * HD)
        pad = jnp.zeros((count - rows - own, HD), BF)
        k = jnp.concatenate([k_ref[:, at], ok_ref[:, at], pad], axis=0)
        v = jnp.concatenate([v_ref[:, at], ov_ref[:, at], pad], axis=0)
        for g in range(group):
            h = kh * group + g
            high, low = two_parts(q_ref[:, h * HD : (h + 1) * HD].astype(F32) * scale)
            s = jnp.where(keep, dot_t(high, k) + dot_t(low, k), BELOW)
            top = jnp.maximum(jnp.max(s, axis=1, keepdims=True), FLOOR)
            p = jnp.exp2(s - top)
            total = jnp.sum(p, axis=1, keepdims=True)
            some = total > 0.0
            o = dot(p.astype(BF), v) / jnp.where(some, total, 1.0)
            out_ref[:, h * HD : (h + 1) * HD] = o.astype(BF)
            size = jnp.where(some, top + jnp.log2(jnp.where(some, total, 1.0)), FLOOR)
            high, low = two_parts(size)
            tail = jnp.where(lane == h, high.astype(F32), tail)
            tail = jnp.where(lane == h + 64, low.astype(F32), tail)
    width = kv_heads * group * HD
    out_ref[:, width : width + HD] = tail.astype(BF)


def states(shape, q, k, v, own_k, own_v, keep):
    vmem = pl.BlockSpec(memory_space=pltpu.VMEM)
    return pl.pallas_call(
        functools.partial(state_kernel, shape),
        out_shape=jax.ShapeDtypeStruct((q.shape[0], q.shape[1] + HD), BF),
        in_specs=[vmem] * 6,
        out_specs=vmem,
        compiler_params=pltpu.CompilerParams(vmem_limit_bytes=32 * 2**20),
        cost_estimate=pl.CostEstimate(flops=1_000_000_000, bytes_accessed=1_500_000, transcendentals=400_000),
    )(q, k, v, own_k, own_v, keep)


def swap(value, axis):
    return lax.ppermute(value, axis, [(0, 1), (1, 0)])


def local(
    prefill_queries,
    prefill_keys,
    prefill_values,
    segments,
    decode_queries,
    decode_keys,
    decode_values,
    row_request,
    norm_gain,
    head_weight,
    allowed_tiles,
    tokens,
):
    nz, ny, nx = (lax.axis_size(a) for a in CTX)
    nctx = nz * ny * nx
    z, yl, x = (lax.axis_index(a) for a in CTX)
    yh, core = (lax.axis_index(a) for a in TP)
    me = (z * ny + yl) * nx + x
    rows = prefill_queries.shape[0]
    kv_heads = prefill_keys.shape[1] // HD
    width = prefill_queries.shape[1]
    group = width // HD // kv_heads
    half = width // 2
    steps, lines, _ = decode_queries.shape
    model = width * lax.axis_size(TP)

    requests = jnp.arange(8, dtype=jnp.int32)
    begins = jnp.sum((segments[None, :] < requests[:, None]).astype(jnp.int32), axis=1)

    own_segment = lax.dynamic_slice_in_dim(segments, me * rows, rows)
    line_of = jnp.arange(steps * lines, dtype=jnp.int32) % lines
    step_of = jnp.arange(steps * lines, dtype=jnp.int32) // lines
    request_of = jnp.tile(row_request, steps)
    own_lines = decode_keys.shape[1]
    count = 256
    slot = jnp.arange(count, dtype=jnp.int32) - rows
    key_segment = jnp.concatenate([own_segment, jnp.full((count - rows,), -1, jnp.int32)])
    keep = (request_of[:, None] == key_segment[None, :]) | (
        (line_of[:, None] == me) & (slot[None, :] >= 0) & (slot[None, :] <= step_of[:, None])
    )
    own_k = jnp.pad(decode_keys[:, 0], ((0, 16 - steps), (0, 0)))
    own_v = jnp.pad(decode_values[:, 0], ((0, 16 - steps), (0, 0)))
    state = states(
        (steps, lines, kv_heads, group),
        decode_queries.reshape(steps * lines, width),
        prefill_keys,
        prefill_values,
        own_k,
        own_v,
        keep.astype(jnp.int32),
    )
    state = state.reshape(steps, lines, width + HD).transpose(1, 0, 2)

    def mine_and_other(a, w):
        first, second = a[:, :w], a[:, w:]
        return jnp.where(yl == 0, first, second), jnp.where(yl == 0, second, first)

    k_mine, k_other = mine_and_other(prefill_keys, HD)
    v_mine, v_other = mine_and_other(prefill_values, HD)
    got = swap(jnp.stack([k_other, v_other]), "yl")

    def both(mine, other):
        return jnp.where(yl == 0, jnp.stack([mine, other]), jnp.stack([other, mine]))

    k_pair, v_pair = both(k_mine, got[0]), both(v_mine, got[1])
    kv_all = lax.all_gather(jnp.stack([k_pair, v_pair]), ("z", "x"), axis=0)
    q_mine, q_other = mine_and_other(prefill_queries, half)
    q_pair = both(q_mine, swap(q_other, "yl"))

    inside = jnp.arange(rows, dtype=jnp.int32)
    places, starts, infos = [], [], []
    for y in range(ny):
        base = ((z * ny + y) * nx + x) * rows
        place = base + inside
        segment = lax.dynamic_slice_in_dim(segments, base, rows)
        start = jnp.sum(jnp.where(segment[:, None] == requests[None, :], begins[None, :], 0), axis=1)
        places.append(place)
        starts.append(start)
        low, high = jnp.min(start), jnp.max(start)
        infos.append(
            jnp.stack([low // KT, (base + rows - 1) // KT + 1, (high + KT - 1) // KT, (base + 1) // KT])
        )
    output = attend(
        (nz, ny, nx),
        jnp.stack(infos),
        q_pair,
        jnp.stack(starts)[..., None],
        jnp.stack(places)[..., None],
        kv_all,
    )

    met = lax.all_to_all(state, CTX, 0, 0, tiled=True)
    tail = met[:, :, width:].astype(F32)
    heads = kv_heads * group
    size = tail[:, :, 0:heads] + tail[:, :, 64 : 64 + heads]
    share = jnp.exp2(size - jnp.max(size, axis=0))
    share = share / jnp.sum(share, axis=0)
    parts = met[:, :, :width].reshape(nctx, steps, heads, HD).astype(F32)
    attention = jnp.sum(parts * share[..., None], axis=0).reshape(steps, width).astype(BF)

    spread = lax.all_to_all(
        jnp.broadcast_to(attention[None], (nctx, steps, width)), CTX, 0, 0, tiled=True
    ).reshape(lines * steps, width)
    widened = spread.astype(F32)
    squares = jnp.sum(widened * widened, axis=1, keepdims=True)
    scaled = (widened * norm_gain).astype(BF)
    partial_logits = dot(scaled, head_weight)
    span = partial_logits.shape[1]

    def fold(logits, squares, axis, mine):
        wide = logits.shape[1] // 2
        first, second = logits[:, :wide], logits[:, wide:]
        high, low = two_parts(squares)
        lane = lax.broadcasted_iota(jnp.int32, (squares.shape[0], HD), 1)
        extra = jnp.where(lane == 0, high, jnp.where(lane == 1, low, jnp.zeros((), BF)))
        sent = jnp.where(mine == 0, second, first).astype(BF)
        there = swap(jnp.concatenate([sent, extra], axis=1), axis).astype(F32)
        kept = jnp.where(mine == 0, first, second)
        total = squares + there[:, wide : wide + 1] + there[:, wide + 1 : wide + 2]
        return kept + there[:, :wide], total

    logits, squares = fold(partial_logits, squares, "core", core)
    logits, squares = fold(logits, squares, "yh", yh)
    logits = lax.rsqrt(squares / model + EPS) * logits

    quarter = span // 4
    first_id = me * span + core * (span // 2) + yh * quarter
    tiles = first_id // TILE + jnp.arange(quarter // TILE, dtype=jnp.int32)
    allowed = jnp.any(allowed_tiles[..., None] == tiles, axis=2)
    allowed = allowed.transpose(1, 0, 2).reshape(lines * steps, quarter // TILE)
    wanted = tokens.T.reshape(lines * steps, 1) - first_id
    keep_ids = jnp.repeat(allowed, TILE, axis=1)
    masked = jnp.where(keep_ids, logits, FLOOR)
    top = jnp.max(masked, axis=1)
    mass = jnp.sum(jnp.where(keep_ids, jnp.exp(masked - top[:, None]), 0.0), axis=1)
    ids = jnp.arange(quarter, dtype=jnp.int32)
    target = jnp.sum(jnp.where(ids[None, :] == wanted, logits, 0.0), axis=1)

    def joined(top, mass, target, axis):
        peak = jnp.max(top, axis=axis)
        mass = jnp.sum(mass * jnp.exp(top - jnp.expand_dims(peak, axis)), axis=axis)
        return peak, mass, jnp.sum(target, axis=axis)

    stats = jnp.stack([top, mass, target], axis=-1).reshape(lines, steps * 3)
    stats = lax.all_to_all(stats, CTX, 0, 0, tiled=True).reshape(nctx, steps, 3)
    stats = jnp.stack(joined(*(stats[..., i] for i in range(3)), 0))
    stats = lax.all_gather(stats, TP, axis=0)
    top, mass, target = joined(*(stats[:, i] for i in range(3)), 0)
    result = target - (top + jnp.log(mass))

    mine, other = output[0], output[1]
    back = swap(jnp.where(yl == 0, other, mine), "yl")
    kept = jnp.where(yl == 0, mine, other)
    prefill_output = jnp.where(
        yl == 0, jnp.concatenate([kept, back], axis=1), jnp.concatenate([back, kept], axis=1)
    )
    return prefill_output, result[:, None]


def solution(mesh):
    fine = Mesh(mesh.devices.reshape(8, 2, 4, 2, 2), CTX + TP)
    placed = (
        P(CTX, TP),
        P(CTX, TP),
        P(CTX, TP),
        P(),
        P(None, None, TP),
        P(None, CTX, TP),
        P(None, CTX, TP),
        P(),
        P(TP),
        P(TP, CTX),
        P(),
        P(),
    )
    return jax.shard_map(
        local, mesh=fine, in_specs=placed, out_specs=(P(CTX, TP), P(None, CTX)), check_vma=False
    )
```

```python
import functools
import math

import jax
import jax.numpy as jnp
from jax import lax
from jax.experimental import pallas as pl
from jax.experimental.pallas import tpu as pltpu
from jax.sharding import Mesh, PartitionSpec as P

HD = 128
TILE = 128
EPS = 1e-06
FLOOR = -1e30
BELOW = -2e30
LOG2E = 1.4426950408889634
BF = jnp.bfloat16
F32 = jnp.float32
CTX = ("z", "yl", "x")
TP = ("yh", "core")
CHUNK = 320
REQUESTS = 8


def dot_t(a, b):
    return lax.dot_general(a, b, (((1,), (1,)), ((), ())), preferred_element_type=F32)


def dot(a, b):
    return lax.dot_general(a, b, (((1,), (0,)), ((), ())), preferred_element_type=F32)


def two_parts(value):
    high = value.astype(BF)
    return high, (value - high.astype(F32)).astype(BF)


def bound(plan, at, big):
    return functools.reduce(
        jnp.minimum, [jnp.where(plan[2 + i] > at, plan[2 + i], big) for i in range(REQUESTS)]
    )


def attend_kernel(plan, q_ref, row_ref, k_ref, v_ref, out_ref, qs, peak, acc):
    rows, width = q_ref.shape
    group = width // HD
    keys = k_ref.shape[1] * rows
    step = pl.program_id(0)
    first_row = plan[1]

    @pl.when(step == 0)
    def _():
        for h in range(group):
            q = q_ref[:, h * HD : (h + 1) * HD].astype(F32) * (HD**-0.5 * LOG2E)
            high, low = two_parts(q)
            qs[h * rows : (h + 1) * rows, 0:HD] = high
            qs[h * rows : (h + 1) * rows, HD:] = low
        peak[...] = jnp.full(peak.shape, FLOOR, F32)
        acc[...] = jnp.zeros(acc.shape, F32)

    base = (plan[0] + step) * keys

    def part(masked):
        block = (keys, HD)
        k = k_ref[0, :, 0, 0].reshape(block).T
        k = jnp.concatenate([k, k], axis=0)
        v = jnp.concatenate([v_ref[0, :, 0, 0].reshape(block), jnp.ones(block, BF)], axis=1)
        if masked:
            at = base + lax.broadcasted_iota(jnp.int32, (1, keys), 1)
            end = bound(plan, at, 2**30) - first_row
            at = at - first_row
        count = qs.shape[0] // CHUNK
        ahead = dot(qs[0:CHUNK], k)
        for i in range(count):
            s = ahead
            if i + 1 < count:
                ahead = dot(qs[(i + 1) * CHUNK : (i + 2) * CHUNK], k)
            here = slice(i * CHUNK, (i + 1) * CHUNK)
            if masked:
                row = row_ref[here]
                s = jnp.where((at <= row) & (row < end), s, BELOW)
            old = peak[here]
            new = jnp.maximum(old, jnp.max(s, axis=1, keepdims=True))
            peak[here] = new
            p = jnp.exp2(s - new).astype(BF)
            acc[here] = acc[here] * jnp.exp2(old - new) + dot(p, v)

    last = base + keys - 1
    last_row = first_row + rows - 1
    need = (bound(plan, last, 2**30) > first_row) & (base <= last_row)
    inside = (last <= first_row) & (bound(plan, base, 2**30) > last_row)
    pl.when(need & inside)(functools.partial(part, False))
    pl.when(need & jnp.logical_not(inside))(functools.partial(part, True))

    @pl.when(step == pl.num_programs(0) - 1)
    def _():
        for h in range(group):
            here = slice(h * rows, (h + 1) * rows)
            out_ref[:, h * HD : (h + 1) * HD] = (acc[here, 0:HD] / acc[here, HD:]).astype(BF)


def attend(plan, q, row, kv):
    rows, width = q.shape
    nz, nx, _, ny, _, _ = kv.shape

    def whole(shape):
        return pl.BlockSpec(shape, lambda i, plan: (0,) * len(shape))

    def tiles(kind):
        def index(i, plan):
            at = jnp.minimum(plan[0] + i, (plan[1] + rows - 1) // (nx * rows))
            return (at // ny, 0, kind, at % ny, 0, 0)

        return pl.BlockSpec((1, nx, 1, 1, rows, HD), index)

    flat = width // HD * rows
    return pl.pallas_call(
        attend_kernel,
        out_shape=jax.ShapeDtypeStruct(q.shape, BF),
        grid_spec=pltpu.PrefetchScalarGridSpec(
            num_scalar_prefetch=1,
            grid=(nz * ny,),
            in_specs=[whole(q.shape), whole(row.shape), tiles(0), tiles(1)],
            out_specs=whole(q.shape),
            scratch_shapes=[
                pltpu.VMEM((flat, 2 * HD), BF),
                pltpu.VMEM((flat, 1), F32),
                pltpu.VMEM((flat, 2 * HD), F32),
            ],
        ),
        compiler_params=pltpu.CompilerParams(
            vmem_limit_bytes=24 * 2**20, dimension_semantics=("arbitrary",)
        ),
        cost_estimate=pl.CostEstimate(
            flops=15_000_000_000, bytes_accessed=8_000_000, transcendentals=5_000_000
        ),
    )(plan, q, row, kv, kv)


def merge_kernel(met_ref, out_ref):
    width = out_ref.shape[2]
    tail = met_ref[:, :, width:].astype(F32)
    size = tail + pltpu.roll(tail, HD // 2, 2)
    share = jnp.exp2(size - jnp.max(size, axis=0, keepdims=True))
    share = share / jnp.sum(share, axis=0, keepdims=True)
    for h in range(width // HD):
        here = slice(h * HD, (h + 1) * HD)
        total = jnp.sum(met_ref[:, :, here].astype(F32) * share[:, :, h : h + 1], axis=0, keepdims=True)
        out_ref[:, :, here] = jnp.broadcast_to(total.astype(BF), (out_ref.shape[0], out_ref.shape[1], HD))


def merge(met):
    vmem = pl.BlockSpec(memory_space=pltpu.VMEM)
    return pl.pallas_call(
        merge_kernel,
        out_shape=jax.ShapeDtypeStruct((met.shape[0], met.shape[1], met.shape[2] - HD), BF),
        in_specs=[vmem],
        out_specs=vmem,
        compiler_params=pltpu.CompilerParams(vmem_limit_bytes=16 * 2**20),
        cost_estimate=pl.CostEstimate(flops=500_000_000, bytes_accessed=1_500_000, transcendentals=0),
    )(met)


def state_kernel(shape, q_ref, k_ref, v_ref, ok_ref, ov_ref, keep_ref, out_ref):
    steps, lines, kv_heads, group = shape
    rows, own = k_ref.shape[0], ok_ref.shape[0]
    count = keep_ref.shape[1]
    scale = HD**-0.5 * LOG2E
    keep = keep_ref[...] > 0
    lane = lax.broadcasted_iota(jnp.int32, (steps * lines, HD), 1)
    tail = jnp.zeros((steps * lines, HD), F32)
    for kh in range(kv_heads):
        at = slice(kh * HD, (kh + 1) * HD)
        pad = jnp.zeros((count - rows - own, HD), BF)
        k = jnp.concatenate([k_ref[:, at], ok_ref[:, at], pad], axis=0)
        v = jnp.concatenate([v_ref[:, at], ov_ref[:, at], pad], axis=0)
        for g in range(group):
            h = kh * group + g
            high, low = two_parts(q_ref[:, h * HD : (h + 1) * HD].astype(F32) * scale)
            s = jnp.where(keep, dot_t(high, k) + dot_t(low, k), BELOW)
            top = jnp.maximum(jnp.max(s, axis=1, keepdims=True), FLOOR)
            p = jnp.exp2(s - top)
            total = jnp.sum(p, axis=1, keepdims=True)
            some = total > 0.0
            o = dot(p.astype(BF), v) / jnp.where(some, total, 1.0)
            out_ref[:, h * HD : (h + 1) * HD] = o.astype(BF)
            size = jnp.where(some, top + jnp.log2(jnp.where(some, total, 1.0)), FLOOR)
            high, low = two_parts(size)
            tail = jnp.where(lane == h, high.astype(F32), tail)
            tail = jnp.where(lane == h + 64, low.astype(F32), tail)
    width = kv_heads * group * HD
    out_ref[:, width : width + HD] = tail.astype(BF)


def states(shape, q, k, v, own_k, own_v, keep):
    vmem = pl.BlockSpec(memory_space=pltpu.VMEM)
    return pl.pallas_call(
        functools.partial(state_kernel, shape),
        out_shape=jax.ShapeDtypeStruct((q.shape[0], q.shape[1] + HD), BF),
        in_specs=[vmem] * 6,
        out_specs=vmem,
        compiler_params=pltpu.CompilerParams(vmem_limit_bytes=16 * 2**20),
        cost_estimate=pl.CostEstimate(flops=4_000_000_000, bytes_accessed=1_500_000, transcendentals=400_000),
    )(q, k, v, own_k, own_v, keep)


def after(values):
    return lax.optimization_barrier(values)


def swap(value, axis):
    return lax.ppermute(value, axis, [(0, 1), (1, 0)])


def local(
    prefill_queries,
    prefill_keys,
    prefill_values,
    segments,
    decode_queries,
    decode_keys,
    decode_values,
    row_request,
    norm_gain,
    head_weight,
    allowed_tiles,
    tokens,
):
    nz, ny, nx = (lax.axis_size(a) for a in CTX)
    nctx = nz * ny * nx
    z, yl, x = (lax.axis_index(a) for a in CTX)
    yh, core = (lax.axis_index(a) for a in TP)
    me = (z * ny + yl) * nx + x
    rows = prefill_queries.shape[0]
    kv_heads = prefill_keys.shape[1] // HD
    width = prefill_queries.shape[1]
    group = width // HD // kv_heads
    half = width // 2
    steps, lines, _ = decode_queries.shape
    model = width * lax.axis_size(TP)

    requests = jnp.arange(REQUESTS, dtype=jnp.int32)
    begins = jnp.sum((segments[None, :] < requests[:, None]).astype(jnp.int32), axis=1)

    own_segment = lax.dynamic_slice_in_dim(segments, me * rows, rows)
    line_of = jnp.arange(steps * lines, dtype=jnp.int32) % lines
    step_of = jnp.arange(steps * lines, dtype=jnp.int32) // lines
    request_of = jnp.tile(row_request, steps)
    own_lines = decode_keys.shape[1]
    count = 256
    slot = jnp.arange(count, dtype=jnp.int32) - rows
    key_segment = jnp.concatenate([own_segment, jnp.full((count - rows,), -1, jnp.int32)])
    keep = (request_of[:, None] == key_segment[None, :]) | (
        (line_of[:, None] == me) & (slot[None, :] >= 0) & (slot[None, :] <= step_of[:, None])
    )
    own_k = jnp.pad(decode_keys[:, 0], ((0, 16 - steps), (0, 0)))
    own_v = jnp.pad(decode_values[:, 0], ((0, 16 - steps), (0, 0)))
    state = states(
        (steps, lines, kv_heads, group),
        decode_queries.reshape(steps * lines, width),
        prefill_keys,
        prefill_values,
        own_k,
        own_v,
        keep.astype(jnp.int32),
    )
    state = state.reshape(steps, lines, width + HD).transpose(1, 0, 2)

    def mine_and_other(a, w):
        first, second = a[:, :w], a[:, w:]
        return jnp.where(yl == 0, first, second), jnp.where(yl == 0, second, first)

    k_mine, k_other = mine_and_other(prefill_keys, HD)
    v_mine, v_other = mine_and_other(prefill_values, HD)
    kv_mine = jnp.stack([k_mine, v_mine])
    kv_got = swap(jnp.stack([k_other, v_other]), "yl")
    kv_pair = jnp.where(yl == 0, jnp.stack([kv_mine, kv_got], 1), jnp.stack([kv_got, kv_mine], 1))
    kv_pair, state = after((kv_pair, state))
    kv_all = lax.all_gather(kv_pair, ("z", "x"), axis=0)
    kv_all = kv_all.reshape((nz, nx) + kv_pair.shape)

    met = lax.all_to_all(state, CTX, 0, 0, tiled=True)
    attention = merge(met)
    spread = lax.all_to_all(attention, CTX, 0, 0, tiled=True).reshape(lines * steps, width)

    def mirror(value):
        return lax.ppermute(value, "z", [(i, nz - 1 - i) for i in range(nz)])

    q_own, _ = after((prefill_queries, attention))
    q_mine, q_other = mine_and_other(q_own, half)
    q_near, q_far = swap(q_other, "yl"), mirror(q_mine)
    row = jnp.tile(jnp.arange(rows, dtype=jnp.int32), group)[:, None]

    def plan_of(block):
        first_row = block * rows
        start = jnp.max(jnp.where(begins <= first_row, begins, 0))
        return jnp.concatenate([jnp.stack([start // (nx * rows), first_row]), begins])

    near_plan = plan_of((z * ny + 1 - yl) * nx + x)
    far_plan = plan_of(((nz - 1 - z) * ny + yl) * nx + x)

    widened = spread.astype(F32)
    squares = jnp.sum(widened * widened, axis=1, keepdims=True)
    scaled = (widened * norm_gain).astype(BF)
    partial_logits = dot(scaled, head_weight)
    span = partial_logits.shape[1]

    def fold(logits, squares, axis, mine):
        wide = logits.shape[1] // 2
        first, second = logits[:, :wide], logits[:, wide:]
        high, low = two_parts(squares)
        lane = lax.broadcasted_iota(jnp.int32, (squares.shape[0], HD), 1)
        extra = jnp.where(lane == 0, high, jnp.where(lane == 1, low, jnp.zeros((), BF)))
        sent = jnp.where(mine == 0, second, first).astype(BF)
        there = swap(jnp.concatenate([sent, extra], axis=1), axis).astype(F32)
        kept = jnp.where(mine == 0, first, second)
        total = squares + there[:, wide : wide + 1] + there[:, wide + 1 : wide + 2]
        return kept + there[:, :wide], total

    logits, squares = fold(partial_logits, squares, "core", core)
    logits, squares = fold(logits, squares, "yh", yh)
    logits = lax.rsqrt(squares / model + EPS) * logits

    quarter = span // 4
    first_id = me * span + core * (span // 2) + yh * quarter
    tiles = first_id // TILE + jnp.arange(quarter // TILE, dtype=jnp.int32)
    allowed = jnp.any(allowed_tiles[..., None] == tiles, axis=2)
    allowed = allowed.transpose(1, 0, 2).reshape(lines * steps, quarter // TILE)
    wanted = tokens.T.reshape(lines * steps, 1) - first_id
    keep_ids = jnp.repeat(allowed, TILE, axis=1)
    masked = jnp.where(keep_ids, logits, FLOOR)
    top = jnp.max(masked, axis=1)
    mass = jnp.sum(jnp.where(keep_ids, jnp.exp(masked - top[:, None]), 0.0), axis=1)
    ids = jnp.arange(quarter, dtype=jnp.int32)
    target = jnp.sum(jnp.where(ids[None, :] == wanted, logits, 0.0), axis=1)

    def joined(top, mass, target, axis):
        peak = jnp.max(top, axis=axis)
        mass = jnp.sum(mass * jnp.exp(top - jnp.expand_dims(peak, axis)), axis=axis)
        return peak, mass, jnp.sum(target, axis=axis)

    stats = jnp.stack([top, mass, target], axis=-1).reshape(lines, steps * 3)
    q_far, q_near, stats = after((q_far, q_near, stats))
    far = attend(far_plan, q_far, row, kv_all)
    near = attend(near_plan, q_near, row, kv_all)
    out_mine, out_other = mirror(far), swap(near, "yl")
    stats, _, _ = after((lax.all_to_all(stats, CTX, 0, 0, tiled=True), far, near))
    stats = stats.reshape(nctx, steps, 3)
    stats = jnp.stack(joined(*(stats[..., i] for i in range(3)), 0))
    stats = lax.all_gather(stats, TP, axis=0)
    top, mass, target = joined(*(stats[:, i] for i in range(3)), 0)
    result = target - (top + jnp.log(mass))

    prefill_output = jnp.where(
        yl == 0,
        jnp.concatenate([out_mine, out_other], axis=1),
        jnp.concatenate([out_other, out_mine], axis=1),
    )
    return prefill_output, result[:, None]


def solution(mesh):
    fine = Mesh(mesh.devices.reshape(8, 2, 4, 2, 2), CTX + TP)
    placed = (
        P(CTX, TP),
        P(CTX, TP),
        P(CTX, TP),
        P(),
        P(None, None, TP),
        P(None, CTX, TP),
        P(None, CTX, TP),
        P(),
        P(TP),
        P(TP, CTX),
        P(),
        P(),
    )
    return jax.shard_map(
        local, mesh=fine, in_specs=placed, out_specs=(P(CTX, TP), P(None, CTX)), check_vma=False
    )
```

```python
import functools
import math

import jax
import jax.numpy as jnp
from jax import lax
from jax.experimental import pallas as pl
from jax.experimental.pallas import tpu as pltpu
from jax.sharding import Mesh, PartitionSpec as P

HD = 128
TILE = 128
EPS = 1e-06
FLOOR = -1e30
BELOW = -2e30
LOG2E = 1.4426950408889634
BF = jnp.bfloat16
F32 = jnp.float32
CTX = ("z", "yl", "x")
TP = ("yh", "core")
CHUNK = 320
REQUESTS = 8


def dot_t(a, b):
    return lax.dot_general(a, b, (((1,), (1,)), ((), ())), preferred_element_type=F32)


def dot(a, b):
    return lax.dot_general(a, b, (((1,), (0,)), ((), ())), preferred_element_type=F32)


def two_parts(value):
    high = value.astype(BF)
    return high, (value - high.astype(F32)).astype(BF)


def bound(plan, at):
    return functools.reduce(
        jnp.minimum, [jnp.where(plan[4 + i] > at, plan[4 + i], 2**30) for i in range(REQUESTS)]
    )


def place(plan, step, rows, keys):
    count = lax.div(plan[2] + rows - 1, keys) - lax.div(plan[0], keys) + 1
    which = jnp.where(step >= count, 1, 0)
    tile = jnp.where(step >= count, lax.div(plan[1], keys) + step - count, lax.div(plan[0], keys) + step)
    return which, tile


def attend_kernel(plan, q_ref, row_ref, k_ref, v_ref, out_ref, qs, peak, acc):
    blocks, rows, width = q_ref.shape
    group = width // HD
    keys = k_ref.shape[1] * rows
    step = pl.program_id(0)
    which, tile = place(plan, step, rows, keys)
    first_row = jnp.where(which == 1, plan[3], plan[2])

    @pl.when(step == 0)
    def _():
        for b in range(blocks):
            for h in range(group):
                q = q_ref[b, :, h * HD : (h + 1) * HD].astype(F32) * (HD**-0.5 * LOG2E)
                high, low = two_parts(q)
                qs[b, h * rows : (h + 1) * rows, 0:HD] = high
                qs[b, h * rows : (h + 1) * rows, HD:] = low
        peak[...] = jnp.full(peak.shape, FLOOR, F32)
        acc[...] = jnp.zeros(acc.shape, F32)

    base = tile * keys

    def part(masked):
        block = (keys, HD)
        k = k_ref[0, :, 0, 0].reshape(block).T
        k = jnp.concatenate([k, k], axis=0)
        v = jnp.concatenate([v_ref[0, :, 0, 0].reshape(block), jnp.ones(block, BF)], axis=1)
        if masked:
            at = base + lax.broadcasted_iota(jnp.int32, (1, keys), 1)
            end = bound(plan, at) - first_row
            at = at - first_row
        count = qs.shape[1] // CHUNK
        ahead = dot(qs[which, 0:CHUNK], k)
        for i in range(count):
            s = ahead
            if i + 1 < count:
                ahead = dot(qs[which, (i + 1) * CHUNK : (i + 2) * CHUNK], k)
            here = slice(i * CHUNK, (i + 1) * CHUNK)
            if masked:
                row = row_ref[here]
                s = jnp.where((at <= row) & (row < end), s, BELOW)
            old = peak[which, here]
            new = jnp.maximum(old, jnp.max(s, axis=1, keepdims=True))
            peak[which, here] = new
            p = jnp.exp2(s - new).astype(BF)
            acc[which, here] = acc[which, here] * jnp.exp2(old - new) + dot(p, v)

    last = base + keys - 1
    last_row = first_row + rows - 1
    need = base <= last_row
    inside = (last <= first_row) & (bound(plan, base) > last_row)
    pl.when(need & inside)(functools.partial(part, False))
    pl.when(need & jnp.logical_not(inside))(functools.partial(part, True))

    @pl.when(step == pl.num_programs(0) - 1)
    def _():
        for b in range(blocks):
            for h in range(group):
                here = slice(h * rows, (h + 1) * rows)
                out_ref[b, :, h * HD : (h + 1) * HD] = (acc[b, here, 0:HD] / acc[b, here, HD:]).astype(BF)


def attend(plan, q, row, kv):
    blocks, rows, width = q.shape
    nz, nx, ny, _, _, _ = kv.shape
    keys = nx * rows

    def whole(shape):
        return pl.BlockSpec(shape, lambda i, plan: (0,) * len(shape))

    def tiles(kind):
        def index(i, plan):
            at = jnp.minimum(place(plan, i, rows, keys)[1], nz * ny - 1)
            return (lax.div(at, ny), 0, lax.rem(at, ny), kind, 0, 0)

        return pl.BlockSpec((1, nx, 1, 1, rows, HD), index)

    flat = width // HD * rows
    return pl.pallas_call(
        attend_kernel,
        out_shape=jax.ShapeDtypeStruct(q.shape, BF),
        grid_spec=pltpu.PrefetchScalarGridSpec(
            num_scalar_prefetch=1,
            grid=(nz * ny + 2,),
            in_specs=[whole(q.shape), whole(row.shape), tiles(0), tiles(1)],
            out_specs=whole(q.shape),
            scratch_shapes=[
                pltpu.VMEM((blocks, flat, 2 * HD), BF),
                pltpu.VMEM((blocks, flat, 1), F32),
                pltpu.VMEM((blocks, flat, 2 * HD), F32),
            ],
        ),
        compiler_params=pltpu.CompilerParams(
            vmem_limit_bytes=24 * 2**20, dimension_semantics=("arbitrary",)
        ),
        cost_estimate=pl.CostEstimate(
            flops=20_000_000_000, bytes_accessed=8_000_000, transcendentals=10_000_000
        ),
    )(plan, q, row, kv, kv)


def merge_kernel(met_ref, out_ref):
    width = out_ref.shape[2]
    tail = met_ref[:, :, width:].astype(F32)
    size = tail + pltpu.roll(tail, HD // 2, 2)
    share = jnp.exp2(size - jnp.max(size, axis=0, keepdims=True))
    share = share / jnp.sum(share, axis=0, keepdims=True)
    for h in range(width // HD):
        here = slice(h * HD, (h + 1) * HD)
        total = jnp.sum(met_ref[:, :, here].astype(F32) * share[:, :, h : h + 1], axis=0, keepdims=True)
        out_ref[:, :, here] = jnp.broadcast_to(total.astype(BF), (out_ref.shape[0], out_ref.shape[1], HD))


def merge(met):
    vmem = pl.BlockSpec(memory_space=pltpu.VMEM)
    return pl.pallas_call(
        merge_kernel,
        out_shape=jax.ShapeDtypeStruct((met.shape[0], met.shape[1], met.shape[2] - HD), BF),
        in_specs=[vmem],
        out_specs=vmem,
        compiler_params=pltpu.CompilerParams(vmem_limit_bytes=16 * 2**20),
        cost_estimate=pl.CostEstimate(flops=500_000_000, bytes_accessed=1_500_000, transcendentals=0),
    )(met)


def state_kernel(shape, q_ref, k_ref, v_ref, own_ref, keep_ref, out_ref):
    steps, lines, kv_heads, group = shape
    rows, own = k_ref.shape[0], own_ref.shape[0]
    count = keep_ref.shape[1]
    scale = HD**-0.5 * LOG2E
    keep = keep_ref[...] > 0
    lane = lax.broadcasted_iota(jnp.int32, (steps * lines, HD), 1)
    tail = jnp.zeros((steps * lines, HD), F32)
    for kh in range(kv_heads):
        at = slice(kh * HD, (kh + 1) * HD)
        pad = jnp.zeros((count - rows - own, HD), BF)
        past = slice((kv_heads + kh) * HD, (kv_heads + kh + 1) * HD)
        k = jnp.concatenate([k_ref[:, at], own_ref[:, at], pad], axis=0)
        v = jnp.concatenate([v_ref[:, at], own_ref[:, past], pad], axis=0)
        for g in range(group):
            h = kh * group + g
            high, low = two_parts(q_ref[:, h * HD : (h + 1) * HD].astype(F32) * scale)
            s = jnp.where(keep, dot_t(high, k) + dot_t(low, k), BELOW)
            top = jnp.maximum(jnp.max(s, axis=1, keepdims=True), FLOOR)
            p = jnp.exp2(s - top)
            total = jnp.sum(p, axis=1, keepdims=True)
            some = total > 0.0
            o = dot(p.astype(BF), v) / jnp.where(some, total, 1.0)
            out_ref[:, h * HD : (h + 1) * HD] = o.astype(BF)
            size = jnp.where(some, top + jnp.log2(jnp.where(some, total, 1.0)), FLOOR)
            high, low = two_parts(size)
            tail = jnp.where(lane == h, high.astype(F32), tail)
            tail = jnp.where(lane == h + 64, low.astype(F32), tail)
    width = kv_heads * group * HD
    out_ref[:, width : width + HD] = tail.astype(BF)


def states(shape, q, k, v, own, keep):
    vmem = pl.BlockSpec(memory_space=pltpu.VMEM)
    return pl.pallas_call(
        functools.partial(state_kernel, shape),
        out_shape=jax.ShapeDtypeStruct((q.shape[0], q.shape[1] + HD), BF),
        in_specs=[vmem] * 5,
        out_specs=vmem,
        compiler_params=pltpu.CompilerParams(vmem_limit_bytes=16 * 2**20),
        cost_estimate=pl.CostEstimate(flops=4_000_000_000, bytes_accessed=1_500_000, transcendentals=400_000),
    )(q, k, v, own, keep)


def after(values):
    return lax.optimization_barrier(values)


def swap(value, axis):
    return lax.ppermute(value, axis, [(0, 1), (1, 0)])


def local(
    prefill_queries,
    prefill_keys,
    prefill_values,
    segments,
    decode_queries,
    decode_keys,
    decode_values,
    row_request,
    norm_gain,
    head_weight,
    allowed_tiles,
    tokens,
):
    nz, ny, nx = (lax.axis_size(a) for a in CTX)
    nctx = nz * ny * nx
    z, yl, x = (lax.axis_index(a) for a in CTX)
    yh, core = (lax.axis_index(a) for a in TP)
    me = (z * ny + yl) * nx + x
    rows = prefill_queries.shape[0]
    kv_heads = prefill_keys.shape[1] // HD
    width = prefill_queries.shape[1]
    group = width // HD // kv_heads
    half = width // 2
    steps, lines, _ = decode_queries.shape
    model = width * lax.axis_size(TP)

    requests = jnp.arange(REQUESTS, dtype=jnp.int32)
    begins = jnp.sum((segments[None, :] < requests[:, None]).astype(jnp.int32), axis=1)

    own_segment = lax.dynamic_slice_in_dim(segments, me * rows, rows)
    slot = jnp.arange(256, dtype=jnp.int32)[None, None, :] - rows
    key_segment = jnp.pad(own_segment, (0, 256 - rows), constant_values=-1)[None, None, :]
    line = jnp.arange(lines, dtype=jnp.int32)[None, :, None]
    turn = jnp.arange(steps, dtype=jnp.int32)[:, None, None]
    keep = (row_request[None, :, None] == key_segment) | (
        (line == me) & (slot >= 0) & (slot <= turn)
    )
    def mine_and_other(a, w):
        first, second = a[:, :w], a[:, w:]
        return jnp.where(yl == 0, first, second), jnp.where(yl == 0, second, first)

    k_mine, k_other = mine_and_other(prefill_keys, HD)
    v_mine, v_other = mine_and_other(prefill_values, HD)
    kv_mine = jnp.stack([k_mine, v_mine])
    kv_got = swap(jnp.stack([k_other, v_other]), "yl")
    kv_pair = jnp.where(yl == 0, jnp.stack([kv_mine, kv_got]), jnp.stack([kv_got, kv_mine]))
    def mirror(value):
        return lax.ppermute(value, "z", [(i, nz - 1 - i) for i in range(nz)])

    q_mine, q_other = mine_and_other(prefill_queries, half)
    q_far = mirror(q_mine)

    own = jnp.concatenate([decode_keys[:, 0], decode_values[:, 0]], axis=1)
    state = states(
        (steps, lines, kv_heads, group),
        decode_queries.reshape(steps * lines, width),
        prefill_keys,
        prefill_values,
        jnp.pad(own, ((0, 16 - steps), (0, 0))),
        keep.astype(jnp.int32).reshape(steps * lines, 256),
    )
    state = state.reshape(steps, lines, width + HD).transpose(1, 0, 2)
    kv_pair, state = after((kv_pair, state))
    kv_all = lax.all_gather(kv_pair, ("z", "x"), axis=0).reshape((nz, nx) + kv_pair.shape)

    met = lax.all_to_all(state, CTX, 0, 0, tiled=True)
    met, q_far = after((met, q_far))
    attention = merge(met)
    q_other, attention = after((q_other, attention))
    spread = lax.all_to_all(attention, CTX, 0, 0, tiled=True).reshape(lines * steps, width)

    q_near = swap(q_other, "yl")
    spread, q_near = after((spread, q_near))
    row = jnp.tile(jnp.arange(rows, dtype=jnp.int32), group)[:, None]
    first_rows = jnp.stack([((z * ny + 1 - yl) * nx + x) * rows, ((nz - 1 - z) * ny + yl) * nx * rows + x * rows])
    first_keys = jnp.max(jnp.where(begins[None, :] <= first_rows[:, None], begins[None, :], 0), axis=1)
    plan = jnp.concatenate([first_keys, first_rows, begins])

    widened = spread.astype(F32)
    squares = jnp.sum(widened * widened, axis=1, keepdims=True)
    scaled = (widened * norm_gain).astype(BF)
    partial_logits = dot(scaled, head_weight)
    span = partial_logits.shape[1]

    quarter = span // 4
    high, low = two_parts(squares)
    lane = lax.broadcasted_iota(jnp.int32, (squares.shape[0], 16), 1)
    extra = jnp.where(lane == 0, high, jnp.where(lane == 1, low, jnp.zeros((), BF)))

    def part_of(yh, core):
        return lax.dynamic_slice_in_dim(partial_logits, (core * 2 + yh) * quarter, quarter, 1)

    logits = part_of(yh, core)
    for away in (3, 2, 1):
        sent = part_of(yh ^ (away >> 1), core ^ (away & 1)).astype(BF)
        there = lax.ppermute(
            jnp.concatenate([sent, extra], axis=1), TP, [(i, i ^ away) for i in range(4)]
        )
        logits = logits + there[:, :quarter].astype(F32)
        squares = squares + jnp.sum(there[:, quarter:].astype(F32), axis=1, keepdims=True)
    logits = lax.rsqrt(squares / model + EPS) * logits

    first_id = me * span + core * (span // 2) + yh * quarter
    tiles = first_id // TILE + jnp.arange(quarter // TILE, dtype=jnp.int32)
    allowed = jnp.any(allowed_tiles[..., None] == tiles, axis=2)
    allowed = allowed.transpose(1, 0, 2).reshape(lines * steps, quarter // TILE)
    wanted = tokens.T.reshape(lines * steps, 1) - first_id
    keep_ids = jnp.repeat(allowed, TILE, axis=1)
    masked = jnp.where(keep_ids, logits, FLOOR)
    top = jnp.max(masked, axis=1)
    mass = jnp.sum(jnp.where(keep_ids, jnp.exp(masked - top[:, None]), 0.0), axis=1)
    ids = jnp.arange(quarter, dtype=jnp.int32)
    target = jnp.sum(jnp.where(ids[None, :] == wanted, logits, 0.0), axis=1)

    def joined(top, mass, target, axis):
        peak = jnp.max(top, axis=axis)
        mass = jnp.sum(mass * jnp.exp(top - jnp.expand_dims(peak, axis)), axis=axis)
        return peak, mass, jnp.sum(target, axis=axis)

    stats = jnp.stack([top, mass, target], axis=-1).reshape(lines, steps * 3)
    q_both, stats = after((jnp.stack([q_near, q_far]), stats))
    output = attend(plan, q_both, row, kv_all)
    stats = lax.all_to_all(stats, CTX, 0, 0, tiled=True)
    stats, output = after((stats, output))
    out_other, out_mine = swap(output[0], "yl"), mirror(output[1])
    stats = stats.reshape(nctx, steps, 3)
    stats = jnp.stack(joined(*(stats[..., i] for i in range(3)), 0))
    stats = lax.all_gather(stats, TP, axis=0)
    top, mass, target = joined(*(stats[:, i] for i in range(3)), 0)
    result = target - (top + jnp.log(mass))

    prefill_output = jnp.where(
        yl == 0,
        jnp.concatenate([out_mine, out_other], axis=1),
        jnp.concatenate([out_other, out_mine], axis=1),
    )
    return prefill_output, result[:, None]


def solution(mesh):
    fine = Mesh(mesh.devices.reshape(8, 2, 4, 2, 2), CTX + TP)
    placed = (
        P(CTX, TP),
        P(CTX, TP),
        P(CTX, TP),
        P(),
        P(None, None, TP),
        P(None, CTX, TP),
        P(None, CTX, TP),
        P(),
        P(TP),
        P(TP, CTX),
        P(),
        P(),
    )
    return jax.shard_map(
        local, mesh=fine, in_specs=placed, out_specs=(P(CTX, TP), P(None, CTX)), check_vma=False
    )
```

```python
import functools
import math

import jax
import jax.numpy as jnp
from jax import lax
from jax.experimental import pallas as pl
from jax.experimental.pallas import tpu as pltpu
from jax.sharding import Mesh, PartitionSpec as P

HD = 128
TILE = 128
EPS = 1e-06
FLOOR = -1e30
BELOW = -2e30
LOG2E = 1.4426950408889634
BF = jnp.bfloat16
F32 = jnp.float32
CTX = ("z", "yl", "x")
TP = ("yh", "core")
CHUNK = 320
REQUESTS = 8


def dot_t(a, b):
    return lax.dot_general(a, b, (((1,), (1,)), ((), ())), preferred_element_type=F32)


def dot(a, b):
    return lax.dot_general(a, b, (((1,), (0,)), ((), ())), preferred_element_type=F32)


def two_parts(value):
    high = value.astype(BF)
    return high, (value - high.astype(F32)).astype(BF)


def bound(plan, at):
    return functools.reduce(
        jnp.minimum, [jnp.where(plan[4 + i] > at, plan[4 + i], 2**30) for i in range(REQUESTS)]
    )


def place(plan, step, rows, keys):
    count = lax.div(plan[2] + rows - 1, keys) - lax.div(plan[0], keys) + 1
    which = jnp.where(step >= count, 1, 0)
    tile = jnp.where(step >= count, lax.div(plan[1], keys) + step - count, lax.div(plan[0], keys) + step)
    return which, tile


def attend_kernel(plan, q_ref, row_ref, k_ref, v_ref, out_ref, qs, peak, acc):
    blocks, rows, width = q_ref.shape
    group = width // HD
    keys = k_ref.shape[1] * rows
    step = pl.program_id(0)
    which, tile = place(plan, step, rows, keys)
    first_row = jnp.where(which == 1, plan[3], plan[2])

    @pl.when(step == 0)
    def _():
        for b in range(blocks):
            for h in range(group):
                q = q_ref[b, :, h * HD : (h + 1) * HD].astype(F32) * (HD**-0.5 * LOG2E)
                high, low = two_parts(q)
                qs[b, h * rows : (h + 1) * rows, 0:HD] = high
                qs[b, h * rows : (h + 1) * rows, HD:] = low
        peak[...] = jnp.full(peak.shape, FLOOR, F32)
        acc[...] = jnp.zeros(acc.shape, F32)

    base = tile * keys

    def part(masked):
        block = (keys, HD)
        k = k_ref[0, :, 0, 0].reshape(block).T
        k = jnp.concatenate([k, k], axis=0)
        v = jnp.concatenate([v_ref[0, :, 0, 0].reshape(block), jnp.ones(block, BF)], axis=1)
        if masked:
            at = base + lax.broadcasted_iota(jnp.int32, (1, keys), 1)
            end = bound(plan, at) - first_row
            at = at - first_row
        count = qs.shape[1] // CHUNK
        ahead = dot(qs[which, 0:CHUNK], k)
        for i in range(count):
            s = ahead
            if i + 1 < count:
                ahead = dot(qs[which, (i + 1) * CHUNK : (i + 2) * CHUNK], k)
            here = slice(i * CHUNK, (i + 1) * CHUNK)
            if masked:
                row = row_ref[here]
                s = jnp.where((at <= row) & (row < end), s, BELOW)
            old = peak[which, here]
            new = jnp.maximum(old, jnp.max(s, axis=1, keepdims=True))
            peak[which, here] = new
            p = jnp.exp2(s - new).astype(BF)
            acc[which, here] = acc[which, here] * jnp.exp2(old - new) + dot(p, v)

    last = base + keys - 1
    last_row = first_row + rows - 1
    need = base <= last_row
    inside = (last <= first_row) & (bound(plan, base) > last_row)
    pl.when(need & inside)(functools.partial(part, False))
    pl.when(need & jnp.logical_not(inside))(functools.partial(part, True))

    @pl.when(step == pl.num_programs(0) - 1)
    def _():
        for b in range(blocks):
            for h in range(group):
                here = slice(h * rows, (h + 1) * rows)
                out_ref[b, :, h * HD : (h + 1) * HD] = (acc[b, here, 0:HD] / acc[b, here, HD:]).astype(BF)


def attend(plan, q, row, kv):
    blocks, rows, width = q.shape
    nz, nx, ny, _, _, _ = kv.shape
    keys = nx * rows

    def whole(shape):
        return pl.BlockSpec(shape, lambda i, plan: (0,) * len(shape))

    def tiles(kind):
        def index(i, plan):
            at = jnp.minimum(place(plan, i, rows, keys)[1], nz * ny - 1)
            return (lax.div(at, ny), 0, lax.rem(at, ny), kind, 0, 0)

        return pl.BlockSpec((1, nx, 1, 1, rows, HD), index)

    flat = width // HD * rows
    return pl.pallas_call(
        attend_kernel,
        out_shape=jax.ShapeDtypeStruct(q.shape, BF),
        grid_spec=pltpu.PrefetchScalarGridSpec(
            num_scalar_prefetch=1,
            grid=(nz * ny + 2,),
            in_specs=[whole(q.shape), whole(row.shape), tiles(0), tiles(1)],
            out_specs=whole(q.shape),
            scratch_shapes=[
                pltpu.VMEM((blocks, flat, 2 * HD), BF),
                pltpu.VMEM((blocks, flat, 1), F32),
                pltpu.VMEM((blocks, flat, 2 * HD), F32),
            ],
        ),
        compiler_params=pltpu.CompilerParams(
            vmem_limit_bytes=58 * 2**20, dimension_semantics=("arbitrary",)
        ),
        cost_estimate=pl.CostEstimate(
            flops=20_000_000_000, bytes_accessed=8_000_000, transcendentals=10_000_000
        ),
    )(plan, q, row, kv, kv)


def merge_kernel(met_ref, out_ref):
    width = out_ref.shape[2]
    tail = met_ref[:, :, width:].astype(F32)
    size = tail + pltpu.roll(tail, HD // 2, 2)
    share = jnp.exp2(size - jnp.max(size, axis=0, keepdims=True))
    share = share / jnp.sum(share, axis=0, keepdims=True)
    for h in range(width // HD):
        here = slice(h * HD, (h + 1) * HD)
        total = jnp.sum(met_ref[:, :, here].astype(F32) * share[:, :, h : h + 1], axis=0, keepdims=True)
        out_ref[:, :, here] = jnp.broadcast_to(total.astype(BF), (out_ref.shape[0], out_ref.shape[1], HD))


def merge(met):
    vmem = pl.BlockSpec(memory_space=pltpu.VMEM)
    return pl.pallas_call(
        merge_kernel,
        out_shape=jax.ShapeDtypeStruct((met.shape[0], met.shape[1], met.shape[2] - HD), BF),
        in_specs=[vmem],
        out_specs=vmem,
        compiler_params=pltpu.CompilerParams(vmem_limit_bytes=16 * 2**20),
        cost_estimate=pl.CostEstimate(flops=500_000_000, bytes_accessed=1_500_000, transcendentals=0),
    )(met)


def state_kernel(shape, q_ref, k_ref, v_ref, own_ref, keep_ref, out_ref):
    steps, lines, kv_heads, group = shape
    rows, own = k_ref.shape[0], own_ref.shape[0]
    count = keep_ref.shape[1]
    scale = HD**-0.5 * LOG2E
    keep = keep_ref[...] > 0
    lane = lax.broadcasted_iota(jnp.int32, (steps * lines, HD), 1)
    tail = jnp.zeros((steps * lines, HD), F32)
    for kh in range(kv_heads):
        at = slice(kh * HD, (kh + 1) * HD)
        pad = jnp.zeros((count - rows - own, HD), BF)
        past = slice((kv_heads + kh) * HD, (kv_heads + kh + 1) * HD)
        k = jnp.concatenate([k_ref[:, at], own_ref[:, at], pad], axis=0)
        v = jnp.concatenate([v_ref[:, at], own_ref[:, past], pad], axis=0)
        for g in range(group):
            h = kh * group + g
            high, low = two_parts(q_ref[:, h * HD : (h + 1) * HD].astype(F32) * scale)
            s = jnp.where(keep, dot_t(high, k) + dot_t(low, k), BELOW)
            top = jnp.maximum(jnp.max(s, axis=1, keepdims=True), FLOOR)
            p = jnp.exp2(s - top)
            total = jnp.sum(p, axis=1, keepdims=True)
            some = total > 0.0
            o = dot(p.astype(BF), v) / jnp.where(some, total, 1.0)
            out_ref[:, h * HD : (h + 1) * HD] = o.astype(BF)
            size = jnp.where(some, top + jnp.log2(jnp.where(some, total, 1.0)), FLOOR)
            high, low = two_parts(size)
            tail = jnp.where(lane == h, high.astype(F32), tail)
            tail = jnp.where(lane == h + 64, low.astype(F32), tail)
    width = kv_heads * group * HD
    out_ref[:, width : width + HD] = tail.astype(BF)


def states(shape, q, k, v, own, keep):
    vmem = pl.BlockSpec(memory_space=pltpu.VMEM)
    return pl.pallas_call(
        functools.partial(state_kernel, shape),
        out_shape=jax.ShapeDtypeStruct((q.shape[0], q.shape[1] + HD), BF),
        in_specs=[vmem] * 5,
        out_specs=vmem,
        compiler_params=pltpu.CompilerParams(vmem_limit_bytes=16 * 2**20),
        cost_estimate=pl.CostEstimate(flops=4_000_000_000, bytes_accessed=1_500_000, transcendentals=400_000),
    )(q, k, v, own, keep)


def after(values):
    return lax.optimization_barrier(values)


def swap(value, axis):
    return lax.ppermute(value, axis, [(0, 1), (1, 0)])


def local(
    prefill_queries,
    prefill_keys,
    prefill_values,
    segments,
    decode_queries,
    decode_keys,
    decode_values,
    row_request,
    norm_gain,
    head_weight,
    allowed_tiles,
    tokens,
):
    nz, ny, nx = (lax.axis_size(a) for a in CTX)
    nctx = nz * ny * nx
    z, yl, x = (lax.axis_index(a) for a in CTX)
    yh, core = (lax.axis_index(a) for a in TP)
    me = (z * ny + yl) * nx + x
    rows = prefill_queries.shape[0]
    kv_heads = prefill_keys.shape[1] // HD
    width = prefill_queries.shape[1]
    group = width // HD // kv_heads
    half = width // 2
    steps, lines, _ = decode_queries.shape
    model = width * lax.axis_size(TP)

    requests = jnp.arange(REQUESTS, dtype=jnp.int32)
    begins = jnp.sum((segments[None, :] < requests[:, None]).astype(jnp.int32), axis=1)

    own_segment = lax.dynamic_slice_in_dim(segments, me * rows, rows)
    slot = jnp.arange(256, dtype=jnp.int32)[None, None, :] - rows
    key_segment = jnp.pad(own_segment, (0, 256 - rows), constant_values=-1)[None, None, :]
    line = jnp.arange(lines, dtype=jnp.int32)[None, :, None]
    turn = jnp.arange(steps, dtype=jnp.int32)[:, None, None]
    keep = (row_request[None, :, None] == key_segment) | (
        (line == me) & (slot >= 0) & (slot <= turn)
    )
    def mine_and_other(a, w):
        first, second = a[:, :w], a[:, w:]
        return jnp.where(yl == 0, first, second), jnp.where(yl == 0, second, first)

    k_mine, k_other = mine_and_other(prefill_keys, HD)
    v_mine, v_other = mine_and_other(prefill_values, HD)
    kv_mine = jnp.stack([k_mine, v_mine])
    kv_got = swap(jnp.stack([k_other, v_other]), "yl")
    kv_pair = jnp.where(yl == 0, jnp.stack([kv_mine, kv_got]), jnp.stack([kv_got, kv_mine]))
    def mirror(value):
        return lax.ppermute(value, "z", [(i, nz - 1 - i) for i in range(nz)])

    q_mine, q_other = mine_and_other(prefill_queries, half)
    q_far = mirror(q_mine)

    own = jnp.concatenate([decode_keys[:, 0], decode_values[:, 0]], axis=1)
    state = states(
        (steps, lines, kv_heads, group),
        decode_queries.reshape(steps * lines, width),
        prefill_keys,
        prefill_values,
        jnp.pad(own, ((0, 16 - steps), (0, 0))),
        keep.astype(jnp.int32).reshape(steps * lines, 256),
    )
    state = state.reshape(steps, lines, width + HD).transpose(1, 0, 2)
    kv_pair, state = after((kv_pair, state))
    kv_all = lax.all_gather(kv_pair, ("z", "x"), axis=0).reshape((nz, nx) + kv_pair.shape)
    state, q_far = after((state, q_far))

    met = lax.all_to_all(state, CTX, 0, 0, tiled=True)
    attention = merge(met)
    q_other, attention = after((q_other, attention))
    spread = lax.all_to_all(attention, CTX, 0, 0, tiled=True).reshape(lines * steps, width)

    q_near = swap(q_other, "yl")
    spread, q_near = after((spread, q_near))
    row = jnp.tile(jnp.arange(rows, dtype=jnp.int32), group)[:, None]
    first_rows = jnp.stack([((z * ny + 1 - yl) * nx + x) * rows, ((nz - 1 - z) * ny + yl) * nx * rows + x * rows])
    first_keys = jnp.max(jnp.where(begins[None, :] <= first_rows[:, None], begins[None, :], 0), axis=1)
    plan = jnp.concatenate([first_keys, first_rows, begins])

    widened = spread.astype(F32)
    squares = jnp.sum(widened * widened, axis=1, keepdims=True)
    scaled = (widened * norm_gain).astype(BF)
    partial_logits = dot(scaled, head_weight)
    span = partial_logits.shape[1]

    quarter = span // 4
    high, low = two_parts(squares)
    lane = lax.broadcasted_iota(jnp.int32, (squares.shape[0], 16), 1)
    extra = jnp.where(lane == 0, high, jnp.where(lane == 1, low, jnp.zeros((), BF)))

    def part_of(yh, core):
        return lax.dynamic_slice_in_dim(partial_logits, (core * 2 + yh) * quarter, quarter, 1)

    logits = part_of(yh, core)
    for away in (3, 2, 1):
        sent = part_of(yh ^ (away >> 1), core ^ (away & 1)).astype(BF)
        there = lax.ppermute(
            jnp.concatenate([sent, extra], axis=1), TP, [(i, i ^ away) for i in range(4)]
        )
        logits = logits + there[:, :quarter].astype(F32)
        squares = squares + jnp.sum(there[:, quarter:].astype(F32), axis=1, keepdims=True)
    logits = lax.rsqrt(squares / model + EPS) * logits

    first_id = me * span + core * (span // 2) + yh * quarter
    tiles = first_id // TILE + jnp.arange(quarter // TILE, dtype=jnp.int32)
    allowed = jnp.any(allowed_tiles[..., None] == tiles, axis=2)
    allowed = allowed.transpose(1, 0, 2).reshape(lines * steps, quarter // TILE)
    wanted = tokens.T.reshape(lines * steps, 1) - first_id
    keep_ids = jnp.repeat(allowed, TILE, axis=1)
    masked = jnp.where(keep_ids, logits, FLOOR)
    top = jnp.max(masked, axis=1)
    mass = jnp.sum(jnp.where(keep_ids, jnp.exp(masked - top[:, None]), 0.0), axis=1)
    ids = jnp.arange(quarter, dtype=jnp.int32)
    target = jnp.sum(jnp.where(ids[None, :] == wanted, logits, 0.0), axis=1)

    def joined(top, mass, target, axis):
        peak = jnp.max(top, axis=axis)
        mass = jnp.sum(mass * jnp.exp(top - jnp.expand_dims(peak, axis)), axis=axis)
        return peak, mass, jnp.sum(target, axis=axis)

    stats = jnp.stack([top, mass, target], axis=-1).reshape(lines, steps * 3)
    q_both, stats = after((jnp.stack([q_near, q_far]), stats))
    output = attend(plan, q_both, row, kv_all)
    stats = lax.all_to_all(stats, CTX, 0, 0, tiled=True)
    stats, output = after((stats, output))
    out_other, out_mine = swap(output[0], "yl"), mirror(output[1])
    stats = stats.reshape(nctx, steps, 3)
    stats = jnp.stack(joined(*(stats[..., i] for i in range(3)), 0))
    stats = lax.all_gather(stats, TP, axis=0)
    top, mass, target = joined(*(stats[:, i] for i in range(3)), 0)
    result = target - (top + jnp.log(mass))

    prefill_output = jnp.where(
        yl == 0,
        jnp.concatenate([out_mine, out_other], axis=1),
        jnp.concatenate([out_other, out_mine], axis=1),
    )
    return prefill_output, result[:, None]


def solution(mesh):
    fine = Mesh(mesh.devices.reshape(8, 2, 4, 2, 2), CTX + TP)
    placed = (
        P(CTX, TP),
        P(CTX, TP),
        P(CTX, TP),
        P(),
        P(None, None, TP),
        P(None, CTX, TP),
        P(None, CTX, TP),
        P(),
        P(TP),
        P(TP, CTX),
        P(),
        P(),
    )
    return jax.shard_map(
        local, mesh=fine, in_specs=placed, out_specs=(P(CTX, TP), P(None, CTX)), check_vma=False
    )
```

```python
import functools
import math

import jax
import jax.numpy as jnp
from jax import lax
from jax.experimental import pallas as pl
from jax.experimental.pallas import tpu as pltpu
from jax.sharding import Mesh, PartitionSpec as P

HD = 128
TILE = 128
EPS = 1e-06
FLOOR = -1e30
BELOW = -2e30
LOG2E = 1.4426950408889634
BF = jnp.bfloat16
F32 = jnp.float32
CTX = ("z", "yl", "x")
TP = ("yh", "core")
CHUNK = 320
REQUESTS = 8


def dot_t(a, b):
    return lax.dot_general(a, b, (((1,), (1,)), ((), ())), preferred_element_type=F32)


def dot(a, b):
    return lax.dot_general(a, b, (((1,), (0,)), ((), ())), preferred_element_type=F32)


def two_parts(value):
    high = value.astype(BF)
    return high, (value - high.astype(F32)).astype(BF)


def bound(plan, at):
    return functools.reduce(
        jnp.minimum, [jnp.where(plan[4 + i] > at, plan[4 + i], 2**30) for i in range(REQUESTS)]
    )


def place(plan, step, rows, keys):
    count = lax.div(plan[2] + rows - 1, keys) - lax.div(plan[0], keys) + 1
    which = jnp.where(step >= count, 1, 0)
    tile = jnp.where(step >= count, lax.div(plan[1], keys) + step - count, lax.div(plan[0], keys) + step)
    return which, tile


def attend_kernel(plan, qa_ref, qb_ref, row_ref, k_ref, v_ref, outa_ref, outb_ref, qs, peak, acc):
    rows, width = qa_ref.shape
    group = width // HD
    keys = k_ref.shape[1] * rows
    step = pl.program_id(0)
    which, tile = place(plan, step, rows, keys)
    first_row = jnp.where(which == 1, plan[3], plan[2])

    @pl.when(step == 0)
    def _():
        for b, q_ref in enumerate((qa_ref, qb_ref)):
            for h in range(group):
                q = q_ref[:, h * HD : (h + 1) * HD].astype(F32) * (HD**-0.5 * LOG2E)
                high, low = two_parts(q)
                qs[b, h * rows : (h + 1) * rows, 0:HD] = high
                qs[b, h * rows : (h + 1) * rows, HD:] = low
        peak[...] = jnp.full(peak.shape, FLOOR, F32)
        acc[...] = jnp.zeros(acc.shape, F32)

    base = tile * keys

    def part(masked):
        block = (keys, HD)
        k = k_ref[0, :, 0, 0].reshape(block).T
        k = jnp.concatenate([k, k], axis=0)
        v = jnp.concatenate([v_ref[0, :, 0, 0].reshape(block), jnp.ones(block, BF)], axis=1)
        if masked:
            at = base + lax.broadcasted_iota(jnp.int32, (1, keys), 1)
            end = bound(plan, at) - first_row
            at = at - first_row
        count = qs.shape[1] // CHUNK
        ahead = dot(qs[which, 0:CHUNK], k)
        for i in range(count):
            s = ahead
            if i + 1 < count:
                ahead = dot(qs[which, (i + 1) * CHUNK : (i + 2) * CHUNK], k)
            here = slice(i * CHUNK, (i + 1) * CHUNK)
            if masked:
                row = row_ref[here]
                s = jnp.where((at <= row) & (row < end), s, BELOW)
            old = peak[which, here]
            new = jnp.maximum(old, jnp.max(s, axis=1, keepdims=True))
            peak[which, here] = new
            p = jnp.exp2(s - new).astype(BF)
            acc[which, here] = acc[which, here] * jnp.exp2(old - new) + dot(p, v)

    last = base + keys - 1
    last_row = first_row + rows - 1
    need = base <= last_row
    inside = (last <= first_row) & (bound(plan, base) > last_row)
    pl.when(need & inside)(functools.partial(part, False))
    pl.when(need & jnp.logical_not(inside))(functools.partial(part, True))

    @pl.when(step == pl.num_programs(0) - 1)
    def _():
        for b, out_ref in enumerate((outa_ref, outb_ref)):
            for h in range(group):
                here = slice(h * rows, (h + 1) * rows)
                out_ref[:, h * HD : (h + 1) * HD] = (acc[b, here, 0:HD] / acc[b, here, HD:]).astype(BF)


def attend(plan, qa, qb, row, kv):
    rows, width = qa.shape
    nz, nx, ny, _, _, _ = kv.shape
    keys = nx * rows

    def whole(shape):
        return pl.BlockSpec(shape, lambda i, plan: (0,) * len(shape))

    def tiles(kind):
        def index(i, plan):
            at = jnp.minimum(place(plan, i, rows, keys)[1], nz * ny - 1)
            return (lax.div(at, ny), 0, lax.rem(at, ny), kind, 0, 0)

        return pl.BlockSpec((1, nx, 1, 1, rows, HD), index)

    flat = width // HD * rows
    return pl.pallas_call(
        attend_kernel,
        out_shape=[jax.ShapeDtypeStruct(qa.shape, BF)] * 2,
        grid_spec=pltpu.PrefetchScalarGridSpec(
            num_scalar_prefetch=1,
            grid=(nz * ny + 2,),
            in_specs=[whole(qa.shape), whole(qb.shape), whole(row.shape), tiles(0), tiles(1)],
            out_specs=[whole(qa.shape)] * 2,
            scratch_shapes=[
                pltpu.VMEM((2, flat, 2 * HD), BF),
                pltpu.VMEM((2, flat, 1), F32),
                pltpu.VMEM((2, flat, 2 * HD), F32),
            ],
        ),
        compiler_params=pltpu.CompilerParams(
            vmem_limit_bytes=58 * 2**20, dimension_semantics=("arbitrary",)
        ),
        cost_estimate=pl.CostEstimate(
            flops=20_000_000_000, bytes_accessed=8_000_000, transcendentals=10_000_000
        ),
    )(plan, qa, qb, row, kv, kv)


def merge_kernel(met_ref, out_ref):
    width = out_ref.shape[2]
    tail = met_ref[:, :, width:].astype(F32)
    size = tail + pltpu.roll(tail, HD // 2, 2)
    share = jnp.exp2(size - jnp.max(size, axis=0, keepdims=True))
    share = share / jnp.sum(share, axis=0, keepdims=True)
    for h in range(width // HD):
        here = slice(h * HD, (h + 1) * HD)
        total = jnp.sum(met_ref[:, :, here].astype(F32) * share[:, :, h : h + 1], axis=0, keepdims=True)
        out_ref[:, :, here] = jnp.broadcast_to(total.astype(BF), (out_ref.shape[0], out_ref.shape[1], HD))


def merge(met):
    vmem = pl.BlockSpec(memory_space=pltpu.VMEM)
    return pl.pallas_call(
        merge_kernel,
        out_shape=jax.ShapeDtypeStruct((met.shape[0], met.shape[1], met.shape[2] - HD), BF),
        in_specs=[vmem],
        out_specs=vmem,
        compiler_params=pltpu.CompilerParams(vmem_limit_bytes=16 * 2**20),
        cost_estimate=pl.CostEstimate(flops=500_000_000, bytes_accessed=1_500_000, transcendentals=0),
    )(met)


def state_kernel(shape, q_ref, k_ref, v_ref, own_ref, keep_ref, out_ref):
    steps, lines, kv_heads, group = shape
    rows, own = k_ref.shape[0], own_ref.shape[0]
    count = keep_ref.shape[1]
    scale = HD**-0.5 * LOG2E
    keep = keep_ref[...] > 0
    lane = lax.broadcasted_iota(jnp.int32, (steps * lines, HD), 1)
    tail = jnp.zeros((steps * lines, HD), F32)
    for kh in range(kv_heads):
        at = slice(kh * HD, (kh + 1) * HD)
        pad = jnp.zeros((count - rows - own, HD), BF)
        past = slice((kv_heads + kh) * HD, (kv_heads + kh + 1) * HD)
        k = jnp.concatenate([k_ref[:, at], own_ref[:, at], pad], axis=0)
        v = jnp.concatenate([v_ref[:, at], own_ref[:, past], pad], axis=0)
        for g in range(group):
            h = kh * group + g
            high, low = two_parts(q_ref[:, h * HD : (h + 1) * HD].astype(F32) * scale)
            s = jnp.where(keep, dot_t(high, k) + dot_t(low, k), BELOW)
            top = jnp.maximum(jnp.max(s, axis=1, keepdims=True), FLOOR)
            p = jnp.exp2(s - top)
            total = jnp.sum(p, axis=1, keepdims=True)
            some = total > 0.0
            o = dot(p.astype(BF), v) / jnp.where(some, total, 1.0)
            out_ref[:, h * HD : (h + 1) * HD] = o.astype(BF)
            size = jnp.where(some, top + jnp.log2(jnp.where(some, total, 1.0)), FLOOR)
            high, low = two_parts(size)
            tail = jnp.where(lane == h, high.astype(F32), tail)
            tail = jnp.where(lane == h + 64, low.astype(F32), tail)
    width = kv_heads * group * HD
    out_ref[:, width : width + HD] = tail.astype(BF)


def states(shape, q, k, v, own, keep):
    vmem = pl.BlockSpec(memory_space=pltpu.VMEM)
    return pl.pallas_call(
        functools.partial(state_kernel, shape),
        out_shape=jax.ShapeDtypeStruct((q.shape[0], q.shape[1] + HD), BF),
        in_specs=[vmem] * 5,
        out_specs=vmem,
        compiler_params=pltpu.CompilerParams(vmem_limit_bytes=16 * 2**20),
        cost_estimate=pl.CostEstimate(flops=4_000_000_000, bytes_accessed=1_500_000, transcendentals=400_000),
    )(q, k, v, own, keep)


def after(values):
    return lax.optimization_barrier(values)


def swap(value, axis):
    return lax.ppermute(value, axis, [(0, 1), (1, 0)])


def local(
    prefill_queries,
    prefill_keys,
    prefill_values,
    segments,
    decode_queries,
    decode_keys,
    decode_values,
    row_request,
    norm_gain,
    head_weight,
    allowed_tiles,
    tokens,
):
    nz, ny, nx = (lax.axis_size(a) for a in CTX)
    nctx = nz * ny * nx
    z, yl, x = (lax.axis_index(a) for a in CTX)
    yh, core = (lax.axis_index(a) for a in TP)
    me = (z * ny + yl) * nx + x
    rows = prefill_queries.shape[0]
    kv_heads = prefill_keys.shape[1] // HD
    width = prefill_queries.shape[1]
    group = width // HD // kv_heads
    half = width // 2
    steps, lines, _ = decode_queries.shape
    model = width * lax.axis_size(TP)

    requests = jnp.arange(REQUESTS, dtype=jnp.int32)
    begins = jnp.sum((segments[None, :] < requests[:, None]).astype(jnp.int32), axis=1)

    own_segment = lax.dynamic_slice_in_dim(segments, me * rows, rows)
    slot = jnp.arange(256, dtype=jnp.int32)[None, None, :] - rows
    key_segment = jnp.pad(own_segment, (0, 256 - rows), constant_values=-1)[None, None, :]
    line = jnp.arange(lines, dtype=jnp.int32)[None, :, None]
    turn = jnp.arange(steps, dtype=jnp.int32)[:, None, None]
    keep = (row_request[None, :, None] == key_segment) | (
        (line == me) & (slot >= 0) & (slot <= turn)
    )
    def mine_and_other(a, w):
        first, second = a[:, :w], a[:, w:]
        return jnp.where(yl == 0, first, second), jnp.where(yl == 0, second, first)

    k_mine, k_other = mine_and_other(prefill_keys, HD)
    v_mine, v_other = mine_and_other(prefill_values, HD)
    kv_mine = jnp.stack([k_mine, v_mine])
    kv_got = swap(jnp.stack([k_other, v_other]), "yl")
    kv_pair = jnp.where(yl == 0, jnp.stack([kv_mine, kv_got]), jnp.stack([kv_got, kv_mine]))
    def mirror(value):
        return lax.ppermute(value, "z", [(i, nz - 1 - i) for i in range(nz)])

    q_mine, q_other = mine_and_other(prefill_queries, half)
    q_far = mirror(q_mine)

    own = jnp.concatenate([decode_keys[:, 0], decode_values[:, 0]], axis=1)
    state = states(
        (steps, lines, kv_heads, group),
        decode_queries.reshape(steps * lines, width),
        prefill_keys,
        prefill_values,
        jnp.pad(own, ((0, 16 - steps), (0, 0))),
        keep.astype(jnp.int32).reshape(steps * lines, 256),
    )
    state = state.reshape(steps, lines, width + HD).transpose(1, 0, 2)
    kv_pair, state, q_far = after((kv_pair, state, q_far))
    kv_all = lax.all_gather(kv_pair, ("z", "x"), axis=0).reshape((nz, nx) + kv_pair.shape)

    met = lax.all_to_all(state, CTX, 0, 0, tiled=True)
    attention = merge(met)
    q_other, attention = after((q_other, attention))
    spread = lax.all_to_all(attention, CTX, 0, 0, tiled=True).reshape(lines * steps, width)

    q_near = swap(q_other, "yl")
    spread, q_near = after((spread, q_near))
    row = jnp.tile(jnp.arange(rows, dtype=jnp.int32), group)[:, None]
    first_rows = jnp.stack([((z * ny + 1 - yl) * nx + x) * rows, ((nz - 1 - z) * ny + yl) * nx * rows + x * rows])
    first_keys = jnp.max(jnp.where(begins[None, :] <= first_rows[:, None], begins[None, :], 0), axis=1)
    plan = jnp.concatenate([first_keys, first_rows, begins])

    widened = spread.astype(F32)
    squares = jnp.sum(widened * widened, axis=1, keepdims=True)
    scaled = (widened * norm_gain).astype(BF)
    partial_logits = dot(scaled, head_weight)
    span = partial_logits.shape[1]

    quarter = span // 4
    high, low = two_parts(squares)
    lane = lax.broadcasted_iota(jnp.int32, (squares.shape[0], 16), 1)
    extra = jnp.where(lane == 0, high, jnp.where(lane == 1, low, jnp.zeros((), BF)))

    def part_of(yh, core):
        return lax.dynamic_slice_in_dim(partial_logits, (core * 2 + yh) * quarter, quarter, 1)

    logits = part_of(yh, core)
    for away in (3, 2, 1):
        sent = part_of(yh ^ (away >> 1), core ^ (away & 1)).astype(BF)
        there = lax.ppermute(
            jnp.concatenate([sent, extra], axis=1), TP, [(i, i ^ away) for i in range(4)]
        )
        logits = logits + there[:, :quarter].astype(F32)
        squares = squares + jnp.sum(there[:, quarter:].astype(F32), axis=1, keepdims=True)
    logits = lax.rsqrt(squares / model + EPS) * logits

    first_id = me * span + core * (span // 2) + yh * quarter
    tiles = first_id // TILE + jnp.arange(quarter // TILE, dtype=jnp.int32)
    allowed = jnp.any(allowed_tiles[..., None] == tiles, axis=2)
    allowed = allowed.transpose(1, 0, 2).reshape(lines * steps, quarter // TILE)
    wanted = tokens.T.reshape(lines * steps, 1) - first_id
    keep_ids = jnp.repeat(allowed, TILE, axis=1)
    masked = jnp.where(keep_ids, logits, FLOOR)
    top = jnp.max(masked, axis=1)
    mass = jnp.sum(jnp.where(keep_ids, jnp.exp(masked - top[:, None]), 0.0), axis=1)
    ids = jnp.arange(quarter, dtype=jnp.int32)
    target = jnp.sum(jnp.where(ids[None, :] == wanted, logits, 0.0), axis=1)

    def joined(top, mass, target, axis):
        peak = jnp.max(top, axis=axis)
        mass = jnp.sum(mass * jnp.exp(top - jnp.expand_dims(peak, axis)), axis=axis)
        return peak, mass, jnp.sum(target, axis=axis)

    stats = jnp.stack([top, mass, target], axis=-1).reshape(lines, steps * 3)
    q_near, q_far, stats = after((q_near, q_far, stats))
    near, far = attend(plan, q_near, q_far, row, kv_all)
    stats = lax.all_to_all(stats, CTX, 0, 0, tiled=True)
    stats, near, far = after((stats, near, far))
    out_other, out_mine = swap(near, "yl"), mirror(far)
    stats = stats.reshape(nctx, steps, 3)
    stats = jnp.stack(joined(*(stats[..., i] for i in range(3)), 0))
    stats = lax.all_gather(stats, TP, axis=0)
    top, mass, target = joined(*(stats[:, i] for i in range(3)), 0)
    result = target - (top + jnp.log(mass))

    prefill_output = jnp.where(
        yl == 0,
        jnp.concatenate([out_mine, out_other], axis=1),
        jnp.concatenate([out_other, out_mine], axis=1),
    )
    return prefill_output, result[:, None]


def solution(mesh):
    fine = Mesh(mesh.devices.reshape(8, 2, 4, 2, 2), CTX + TP)
    placed = (
        P(CTX, TP),
        P(CTX, TP),
        P(CTX, TP),
        P(),
        P(None, None, TP),
        P(None, CTX, TP),
        P(None, CTX, TP),
        P(),
        P(TP),
        P(TP, CTX),
        P(),
        P(),
    )
    return jax.shard_map(
        local, mesh=fine, in_specs=placed, out_specs=(P(CTX, TP), P(None, CTX)), check_vma=False
    )
```

```python
import functools
import math

import jax
import jax.numpy as jnp
from jax import lax
from jax.experimental import pallas as pl
from jax.experimental.pallas import tpu as pltpu
from jax.sharding import Mesh, PartitionSpec as P

HD = 128
TILE = 128
EPS = 1e-06
FLOOR = -1e30
BELOW = -2e30
LOG2E = 1.4426950408889634
BF = jnp.bfloat16
F32 = jnp.float32
CTX = ("z", "yl", "x")
TP = ("yh", "core")
CHUNK = 320
REQUESTS = 8


def dot_t(a, b):
    return lax.dot_general(a, b, (((1,), (1,)), ((), ())), preferred_element_type=F32)


def dot(a, b):
    return lax.dot_general(a, b, (((1,), (0,)), ((), ())), preferred_element_type=F32)


def two_parts(value):
    high = value.astype(BF)
    return high, (value - high.astype(F32)).astype(BF)


def bound(plan, at):
    return functools.reduce(
        jnp.minimum, [jnp.where(plan[4 + i] > at, plan[4 + i], 2**30) for i in range(REQUESTS)]
    )


def place(plan, step, rows, keys):
    count = lax.div(plan[2] + rows - 1, keys) - lax.div(plan[0], keys) + 1
    which = jnp.where(step >= count, 1, 0)
    tile = jnp.where(step >= count, lax.div(plan[1], keys) + step - count, lax.div(plan[0], keys) + step)
    return which, tile


def attend_kernel(plan, qa_ref, qb_ref, row_ref, k_ref, v_ref, outa_ref, outb_ref, qs, peak, acc):
    rows, width = qa_ref.shape
    group = width // HD
    keys = k_ref.shape[1] * rows
    step = pl.program_id(0)
    which, tile = place(plan, step, rows, keys)
    first_row = jnp.where(which == 1, plan[3], plan[2])

    @pl.when(step == 0)
    def _():
        for b, q_ref in enumerate((qa_ref, qb_ref)):
            for h in range(group):
                q = q_ref[:, h * HD : (h + 1) * HD].astype(F32) * (HD**-0.5 * LOG2E)
                high, low = two_parts(q)
                qs[b, h * rows : (h + 1) * rows, 0:HD] = high
                qs[b, h * rows : (h + 1) * rows, HD:] = low
        peak[...] = jnp.full(peak.shape, FLOOR, F32)
        acc[...] = jnp.zeros(acc.shape, F32)

    base = tile * keys

    def part(masked):
        block = (keys, HD)
        k = k_ref[0, :, 0, 0].reshape(block).T
        k = jnp.concatenate([k, k], axis=0)
        v = jnp.concatenate([v_ref[0, :, 0, 0].reshape(block), jnp.ones(block, BF)], axis=1)
        if masked:
            at = base + lax.broadcasted_iota(jnp.int32, (1, keys), 1)
            end = bound(plan, at) - first_row
            at = at - first_row
        count = qs.shape[1] // CHUNK
        ahead = dot(qs[which, 0:CHUNK], k)
        for i in range(count):
            s = ahead
            if i + 1 < count:
                ahead = dot(qs[which, (i + 1) * CHUNK : (i + 2) * CHUNK], k)
            here = slice(i * CHUNK, (i + 1) * CHUNK)
            if masked:
                row = row_ref[here]
                s = jnp.where((at <= row) & (row < end), s, BELOW)
            old = peak[which, here]
            new = jnp.maximum(old, jnp.max(s, axis=1, keepdims=True))
            peak[which, here] = new
            p = jnp.exp2(s - new).astype(BF)
            acc[which, here] = acc[which, here] * jnp.exp2(old - new) + dot(p, v)

    last = base + keys - 1
    last_row = first_row + rows - 1
    need = base <= last_row
    inside = (last <= first_row) & (bound(plan, base) > last_row)
    pl.when(need & inside)(functools.partial(part, False))
    pl.when(need & jnp.logical_not(inside))(functools.partial(part, True))

    @pl.when(step == pl.num_programs(0) - 1)
    def _():
        for b, out_ref in enumerate((outa_ref, outb_ref)):
            for h in range(group):
                here = slice(h * rows, (h + 1) * rows)
                out_ref[:, h * HD : (h + 1) * HD] = (acc[b, here, 0:HD] / acc[b, here, HD:]).astype(BF)


def attend(plan, qa, qb, row, kv):
    rows, width = qa.shape
    nz, nx, ny, _, _, _ = kv.shape
    keys = nx * rows

    def whole(shape):
        return pl.BlockSpec(shape, lambda i, plan: (0,) * len(shape))

    def tiles(kind):
        def index(i, plan):
            at = jnp.minimum(place(plan, i, rows, keys)[1], nz * ny - 1)
            return (lax.div(at, ny), 0, lax.rem(at, ny), kind, 0, 0)

        return pl.BlockSpec((1, nx, 1, 1, rows, HD), index)

    flat = width // HD * rows
    return pl.pallas_call(
        attend_kernel,
        out_shape=[jax.ShapeDtypeStruct(qa.shape, BF)] * 2,
        grid_spec=pltpu.PrefetchScalarGridSpec(
            num_scalar_prefetch=1,
            grid=(nz * ny + 2,),
            in_specs=[whole(qa.shape), whole(qb.shape), whole(row.shape), tiles(0), tiles(1)],
            out_specs=[whole(qa.shape)] * 2,
            scratch_shapes=[
                pltpu.VMEM((2, flat, 2 * HD), BF),
                pltpu.VMEM((2, flat, 1), F32),
                pltpu.VMEM((2, flat, 2 * HD), F32),
            ],
        ),
        compiler_params=pltpu.CompilerParams(
            vmem_limit_bytes=58 * 2**20, dimension_semantics=("arbitrary",)
        ),
        cost_estimate=pl.CostEstimate(
            flops=20_000_000_000, bytes_accessed=8_000_000, transcendentals=10_000_000
        ),
    )(plan, qa, qb, row, kv, kv)


def merge_kernel(met_ref, out_ref):
    width = out_ref.shape[2]
    tail = met_ref[:, :, width:].astype(F32)
    size = tail + pltpu.roll(tail, HD // 2, 2)
    share = jnp.exp2(size - jnp.max(size, axis=0, keepdims=True))
    share = share / jnp.sum(share, axis=0, keepdims=True)
    for h in range(width // HD):
        here = slice(h * HD, (h + 1) * HD)
        total = jnp.sum(met_ref[:, :, here].astype(F32) * share[:, :, h : h + 1], axis=0, keepdims=True)
        out_ref[:, :, here] = jnp.broadcast_to(total.astype(BF), (out_ref.shape[0], out_ref.shape[1], HD))


def merge(met):
    vmem = pl.BlockSpec(memory_space=pltpu.VMEM)
    return pl.pallas_call(
        merge_kernel,
        out_shape=jax.ShapeDtypeStruct((met.shape[0], met.shape[1], met.shape[2] - HD), BF),
        in_specs=[vmem],
        out_specs=vmem,
        compiler_params=pltpu.CompilerParams(vmem_limit_bytes=16 * 2**20),
        cost_estimate=pl.CostEstimate(flops=500_000_000, bytes_accessed=1_500_000, transcendentals=0),
    )(met)


def state_kernel(shape, q_ref, k_ref, v_ref, own_ref, keep_ref, out_ref):
    steps, lines, kv_heads, group = shape
    rows, own = k_ref.shape[0], own_ref.shape[0]
    count = keep_ref.shape[1]
    scale = HD**-0.5 * LOG2E
    keep = keep_ref[...] > 0
    lane = lax.broadcasted_iota(jnp.int32, (steps * lines, HD), 1)
    tail = jnp.zeros((steps * lines, HD), F32)
    for kh in range(kv_heads):
        at = slice(kh * HD, (kh + 1) * HD)
        pad = jnp.zeros((count - rows - own, HD), BF)
        past = slice((kv_heads + kh) * HD, (kv_heads + kh + 1) * HD)
        k = jnp.concatenate([k_ref[:, at], own_ref[:, at], pad], axis=0)
        v = jnp.concatenate([v_ref[:, at], own_ref[:, past], pad], axis=0)
        for g in range(group):
            h = kh * group + g
            high, low = two_parts(q_ref[:, h * HD : (h + 1) * HD].astype(F32) * scale)
            s = jnp.where(keep, dot_t(high, k) + dot_t(low, k), BELOW)
            top = jnp.maximum(jnp.max(s, axis=1, keepdims=True), FLOOR)
            p = jnp.exp2(s - top)
            total = jnp.sum(p, axis=1, keepdims=True)
            some = total > 0.0
            o = dot(p.astype(BF), v) / jnp.where(some, total, 1.0)
            out_ref[:, h * HD : (h + 1) * HD] = o.astype(BF)
            size = jnp.where(some, top + jnp.log2(jnp.where(some, total, 1.0)), FLOOR)
            high, low = two_parts(size)
            tail = jnp.where(lane == h, high.astype(F32), tail)
            tail = jnp.where(lane == h + 64, low.astype(F32), tail)
    width = kv_heads * group * HD
    out_ref[:, width : width + HD] = tail.astype(BF)


def states(shape, q, k, v, own, keep):
    vmem = pl.BlockSpec(memory_space=pltpu.VMEM)
    return pl.pallas_call(
        functools.partial(state_kernel, shape),
        out_shape=jax.ShapeDtypeStruct((q.shape[0], q.shape[1] + HD), BF),
        in_specs=[vmem] * 5,
        out_specs=vmem,
        compiler_params=pltpu.CompilerParams(vmem_limit_bytes=16 * 2**20),
        cost_estimate=pl.CostEstimate(flops=4_000_000_000, bytes_accessed=1_500_000, transcendentals=400_000),
    )(q, k, v, own, keep)


def after(values):
    return lax.optimization_barrier(values)


def swap(value, axis):
    return lax.ppermute(value, axis, [(0, 1), (1, 0)])


def local(
    prefill_queries,
    prefill_keys,
    prefill_values,
    segments,
    decode_queries,
    decode_keys,
    decode_values,
    row_request,
    norm_gain,
    head_weight,
    allowed_tiles,
    tokens,
):
    nz, ny, nx = (lax.axis_size(a) for a in CTX)
    nctx = nz * ny * nx
    z, yl, x = (lax.axis_index(a) for a in CTX)
    yh, core = (lax.axis_index(a) for a in TP)
    me = (z * ny + yl) * nx + x
    rows = prefill_queries.shape[0]
    kv_heads = prefill_keys.shape[1] // HD
    width = prefill_queries.shape[1]
    group = width // HD // kv_heads
    half = width // 2
    steps, lines, _ = decode_queries.shape
    model = width * lax.axis_size(TP)

    requests = jnp.arange(REQUESTS, dtype=jnp.int32)
    begins = jnp.sum((segments[None, :] < requests[:, None]).astype(jnp.int32), axis=1)

    own_segment = lax.dynamic_slice_in_dim(segments, me * rows, rows)
    slot = jnp.arange(256, dtype=jnp.int32)[None, None, :] - rows
    key_segment = jnp.pad(own_segment, (0, 256 - rows), constant_values=-1)[None, None, :]
    line = jnp.arange(lines, dtype=jnp.int32)[None, :, None]
    turn = jnp.arange(steps, dtype=jnp.int32)[:, None, None]
    keep = (row_request[None, :, None] == key_segment) | (
        (line == me) & (slot >= 0) & (slot <= turn)
    )
    def mine_and_other(a, w):
        first, second = a[:, :w], a[:, w:]
        return jnp.where(yl == 0, first, second), jnp.where(yl == 0, second, first)

    k_mine, k_other = mine_and_other(prefill_keys, HD)
    v_mine, v_other = mine_and_other(prefill_values, HD)
    kv_mine = jnp.stack([k_mine, v_mine])
    kv_got = swap(jnp.stack([k_other, v_other]), "yl")
    kv_pair = jnp.where(yl == 0, jnp.stack([kv_mine, kv_got]), jnp.stack([kv_got, kv_mine]))
    def mirror(value):
        return lax.ppermute(value, "z", [(i, nz - 1 - i) for i in range(nz)])

    q_mine, q_other = mine_and_other(prefill_queries, half)
    own = jnp.concatenate([decode_keys[:, 0], decode_values[:, 0]], axis=1)
    own = jnp.pad(own, ((0, 16 - steps), (0, 0)))
    keep = keep.astype(jnp.int32).reshape(steps * lines, 256)
    kv_pair, keep, own, q_mine = after((kv_pair, keep, own, q_mine))
    kv_all = lax.all_gather(kv_pair, ("z", "x"), axis=0).reshape((nz, nx) + kv_pair.shape)
    q_far = mirror(q_mine)
    state = states(
        (steps, lines, kv_heads, group),
        decode_queries.reshape(steps * lines, width),
        prefill_keys,
        prefill_values,
        own,
        keep,
    )
    state = state.reshape(steps, lines, width + HD).transpose(1, 0, 2)
    state, q_far = after((state, q_far))

    met = lax.all_to_all(state, CTX, 0, 0, tiled=True)
    attention = merge(met)
    q_other, attention = after((q_other, attention))
    spread = lax.all_to_all(attention, CTX, 0, 0, tiled=True).reshape(lines * steps, width)

    q_near = swap(q_other, "yl")
    row = jnp.tile(jnp.arange(rows, dtype=jnp.int32), group)[:, None]
    first_rows = jnp.stack([((z * ny + 1 - yl) * nx + x) * rows, ((nz - 1 - z) * ny + yl) * nx * rows + x * rows])
    first_keys = jnp.max(jnp.where(begins[None, :] <= first_rows[:, None], begins[None, :], 0), axis=1)
    plan = jnp.concatenate([first_keys, first_rows, begins])
    spread, q_near, row, plan = after((spread, q_near, row, plan))

    widened = spread.astype(F32)
    squares = jnp.sum(widened * widened, axis=1, keepdims=True)
    scaled = (widened * norm_gain).astype(BF)
    partial_logits = dot(scaled, head_weight)
    span = partial_logits.shape[1]

    quarter = span // 4
    high, low = two_parts(squares)
    lane = lax.broadcasted_iota(jnp.int32, (squares.shape[0], 16), 1)
    extra = jnp.where(lane == 0, high, jnp.where(lane == 1, low, jnp.zeros((), BF)))

    def part_of(yh, core):
        return lax.dynamic_slice_in_dim(partial_logits, (core * 2 + yh) * quarter, quarter, 1)

    logits = part_of(yh, core)
    for away in (3, 2, 1):
        sent = part_of(yh ^ (away >> 1), core ^ (away & 1)).astype(BF)
        there = lax.ppermute(
            jnp.concatenate([sent, extra], axis=1), TP, [(i, i ^ away) for i in range(4)]
        )
        logits = logits + there[:, :quarter].astype(F32)
        squares = squares + jnp.sum(there[:, quarter:].astype(F32), axis=1, keepdims=True)
    logits = lax.rsqrt(squares / model + EPS) * logits

    first_id = me * span + core * (span // 2) + yh * quarter
    tiles = first_id // TILE + jnp.arange(quarter // TILE, dtype=jnp.int32)
    allowed = jnp.any(allowed_tiles[..., None] == tiles, axis=2)
    allowed = allowed.transpose(1, 0, 2).reshape(lines * steps, quarter // TILE)
    wanted = tokens.T.reshape(lines * steps, 1) - first_id
    keep_ids = jnp.repeat(allowed, TILE, axis=1)
    masked = jnp.where(keep_ids, logits, FLOOR)
    top = jnp.max(masked, axis=1)
    mass = jnp.sum(jnp.where(keep_ids, jnp.exp(masked - top[:, None]), 0.0), axis=1)
    ids = jnp.arange(quarter, dtype=jnp.int32)
    target = jnp.sum(jnp.where(ids[None, :] == wanted, logits, 0.0), axis=1)

    def joined(top, mass, target, axis):
        peak = jnp.max(top, axis=axis)
        mass = jnp.sum(mass * jnp.exp(top - jnp.expand_dims(peak, axis)), axis=axis)
        return peak, mass, jnp.sum(target, axis=axis)

    stats = jnp.stack([top, mass, target], axis=-1).reshape(lines, steps * 3)
    q_near, q_far, stats = after((q_near, q_far, stats))
    near, far = attend(plan, q_near, q_far, row, kv_all)
    stats = lax.all_to_all(stats, CTX, 0, 0, tiled=True)
    stats, near, far = after((stats, near, far))
    out_other, out_mine = swap(near, "yl"), mirror(far)
    stats = stats.reshape(nctx, steps, 3)
    stats = jnp.stack(joined(*(stats[..., i] for i in range(3)), 0))
    stats = lax.all_gather(stats, TP, axis=0)
    top, mass, target = joined(*(stats[:, i] for i in range(3)), 0)
    result = target - (top + jnp.log(mass))

    prefill_output = jnp.where(
        yl == 0,
        jnp.concatenate([out_mine, out_other], axis=1),
        jnp.concatenate([out_other, out_mine], axis=1),
    )
    return prefill_output, result[:, None]


def solution(mesh):
    fine = Mesh(mesh.devices.reshape(8, 2, 4, 2, 2), CTX + TP)
    placed = (
        P(CTX, TP),
        P(CTX, TP),
        P(CTX, TP),
        P(),
        P(None, None, TP),
        P(None, CTX, TP),
        P(None, CTX, TP),
        P(),
        P(TP),
        P(TP, CTX),
        P(),
        P(),
    )
    return jax.shard_map(
        local, mesh=fine, in_specs=placed, out_specs=(P(CTX, TP), P(None, CTX)), check_vma=False
    )
```

```python
import functools
import math

import jax
import jax.numpy as jnp
from jax import lax
from jax.experimental import pallas as pl
from jax.experimental.pallas import tpu as pltpu
from jax.sharding import Mesh, PartitionSpec as P

HD = 128
TILE = 128
EPS = 1e-06
FLOOR = -1e30
BELOW = -2e30
LOG2E = 1.4426950408889634
BF = jnp.bfloat16
F32 = jnp.float32
CTX = ("z", "yl", "x")
TP = ("yh", "core")
CHUNK = 320
REQUESTS = 8


def dot_t(a, b):
    return lax.dot_general(a, b, (((1,), (1,)), ((), ())), preferred_element_type=F32)


def dot(a, b):
    return lax.dot_general(a, b, (((1,), (0,)), ((), ())), preferred_element_type=F32)


def two_parts(value):
    high = value.astype(BF)
    return high, (value - high.astype(F32)).astype(BF)


def bound(plan, at):
    return functools.reduce(
        jnp.minimum, [jnp.where(plan[4 + i] > at, plan[4 + i], 2**30) for i in range(REQUESTS)]
    )


def place(plan, step, rows, keys):
    count = lax.div(plan[2] + rows - 1, keys) - lax.div(plan[0], keys) + 1
    which = jnp.where(step >= count, 1, 0)
    tile = jnp.where(step >= count, lax.div(plan[1], keys) + step - count, lax.div(plan[0], keys) + step)
    return which, tile


def attend_kernel(plan, qa_ref, qb_ref, k_ref, v_ref, outa_ref, outb_ref, qs, peak, acc):
    rows, width = qa_ref.shape
    group = width // HD
    keys = k_ref.shape[1] * rows
    step = pl.program_id(0)
    which, tile = place(plan, step, rows, keys)
    first_row = jnp.where(which == 1, plan[3], plan[2])

    @pl.when(step == 0)
    def _():
        for b, q_ref in enumerate((qa_ref, qb_ref)):
            for h in range(group):
                q = q_ref[:, h * HD : (h + 1) * HD].astype(F32) * (HD**-0.5 * LOG2E)
                high, low = two_parts(q)
                qs[b, h * rows : (h + 1) * rows, 0:HD] = high
                qs[b, h * rows : (h + 1) * rows, HD:] = low
        peak[...] = jnp.full(peak.shape, FLOOR, F32)
        acc[...] = jnp.zeros(acc.shape, F32)

    base = tile * keys

    def part(masked):
        block = (keys, HD)
        k = k_ref[0, :, 0, 0].reshape(block).T
        k = jnp.concatenate([k, k], axis=0)
        v = jnp.concatenate([v_ref[0, :, 0, 0].reshape(block), jnp.ones(block, BF)], axis=1)
        if masked:
            at = base + lax.broadcasted_iota(jnp.int32, (1, keys), 1)
            end = bound(plan, at) - first_row
            at = at - first_row
        count = qs.shape[1] // CHUNK
        ahead = dot(qs[which, 0:CHUNK], k)
        for i in range(count):
            s = ahead
            if i + 1 < count:
                ahead = dot(qs[which, (i + 1) * CHUNK : (i + 2) * CHUNK], k)
            here = slice(i * CHUNK, (i + 1) * CHUNK)
            if masked:
                row = i * CHUNK + lax.broadcasted_iota(jnp.int32, (CHUNK, 1), 0)
                row = row - sum(jnp.where(row >= h * rows, rows, 0) for h in range(1, group))
                s = jnp.where((at <= row) & (row < end), s, BELOW)
            old = peak[which, here]
            new = jnp.maximum(old, jnp.max(s, axis=1, keepdims=True))
            peak[which, here] = new
            p = jnp.exp2(s - new).astype(BF)
            acc[which, here] = acc[which, here] * jnp.exp2(old - new) + dot(p, v)

    last = base + keys - 1
    last_row = first_row + rows - 1
    need = base <= last_row
    inside = (last <= first_row) & (bound(plan, base) > last_row)
    pl.when(need & inside)(functools.partial(part, False))
    pl.when(need & jnp.logical_not(inside))(functools.partial(part, True))

    @pl.when(step == pl.num_programs(0) - 1)
    def _():
        for b, out_ref in enumerate((outa_ref, outb_ref)):
            for h in range(group):
                here = slice(h * rows, (h + 1) * rows)
                out_ref[:, h * HD : (h + 1) * HD] = (acc[b, here, 0:HD] / acc[b, here, HD:]).astype(BF)


def attend(plan, qa, qb, kv):
    rows, width = qa.shape
    nz, nx, ny, _, _, _ = kv.shape
    keys = nx * rows

    def whole(shape):
        return pl.BlockSpec(shape, lambda i, plan: (0,) * len(shape))

    def tiles(kind):
        def index(i, plan):
            at = jnp.minimum(place(plan, i, rows, keys)[1], nz * ny - 1)
            return (lax.div(at, ny), 0, lax.rem(at, ny), kind, 0, 0)

        return pl.BlockSpec((1, nx, 1, 1, rows, HD), index)

    flat = width // HD * rows
    return pl.pallas_call(
        attend_kernel,
        out_shape=[jax.ShapeDtypeStruct(qa.shape, BF)] * 2,
        grid_spec=pltpu.PrefetchScalarGridSpec(
            num_scalar_prefetch=1,
            grid=(nz * ny + 2,),
            in_specs=[whole(qa.shape), whole(qb.shape), tiles(0), tiles(1)],
            out_specs=[whole(qa.shape)] * 2,
            scratch_shapes=[
                pltpu.VMEM((2, flat, 2 * HD), BF),
                pltpu.VMEM((2, flat, 1), F32),
                pltpu.VMEM((2, flat, 2 * HD), F32),
            ],
        ),
        compiler_params=pltpu.CompilerParams(
            vmem_limit_bytes=58 * 2**20, dimension_semantics=("arbitrary",)
        ),
        cost_estimate=pl.CostEstimate(
            flops=20_000_000_000, bytes_accessed=8_000_000, transcendentals=10_000_000
        ),
    )(plan, qa, qb, kv, kv)


def merge_kernel(met_ref, out_ref):
    width = out_ref.shape[2]
    tail = met_ref[:, :, width:].astype(F32)
    size = tail + pltpu.roll(tail, HD // 2, 2)
    share = jnp.exp2(size - jnp.max(size, axis=0, keepdims=True))
    share = share / jnp.sum(share, axis=0, keepdims=True)
    for h in range(width // HD):
        here = slice(h * HD, (h + 1) * HD)
        total = jnp.sum(met_ref[:, :, here].astype(F32) * share[:, :, h : h + 1], axis=0, keepdims=True)
        out_ref[:, :, here] = jnp.broadcast_to(total.astype(BF), (out_ref.shape[0], out_ref.shape[1], HD))


def merge(met):
    vmem = pl.BlockSpec(memory_space=pltpu.VMEM)
    return pl.pallas_call(
        merge_kernel,
        out_shape=jax.ShapeDtypeStruct((met.shape[0], met.shape[1], met.shape[2] - HD), BF),
        in_specs=[vmem],
        out_specs=vmem,
        compiler_params=pltpu.CompilerParams(vmem_limit_bytes=16 * 2**20),
        cost_estimate=pl.CostEstimate(flops=500_000_000, bytes_accessed=1_500_000, transcendentals=0),
    )(met)


def state_kernel(shape, q_ref, k_ref, v_ref, own_ref, keep_ref, out_ref):
    steps, lines, kv_heads, group = shape
    rows, own = k_ref.shape[0], own_ref.shape[0]
    count = keep_ref.shape[1]
    scale = HD**-0.5 * LOG2E
    keep = keep_ref[...] > 0
    lane = lax.broadcasted_iota(jnp.int32, (steps * lines, HD), 1)
    tail = jnp.zeros((steps * lines, HD), F32)
    for kh in range(kv_heads):
        at = slice(kh * HD, (kh + 1) * HD)
        pad = jnp.zeros((count - rows - own, HD), BF)
        past = slice((kv_heads + kh) * HD, (kv_heads + kh + 1) * HD)
        k = jnp.concatenate([k_ref[:, at], own_ref[:, at], pad], axis=0)
        v = jnp.concatenate([v_ref[:, at], own_ref[:, past], pad], axis=0)
        for g in range(group):
            h = kh * group + g
            high, low = two_parts(q_ref[:, h * HD : (h + 1) * HD].astype(F32) * scale)
            s = jnp.where(keep, dot_t(high, k) + dot_t(low, k), BELOW)
            top = jnp.maximum(jnp.max(s, axis=1, keepdims=True), FLOOR)
            p = jnp.exp2(s - top)
            total = jnp.sum(p, axis=1, keepdims=True)
            some = total > 0.0
            o = dot(p.astype(BF), v) / jnp.where(some, total, 1.0)
            out_ref[:, h * HD : (h + 1) * HD] = o.astype(BF)
            size = jnp.where(some, top + jnp.log2(jnp.where(some, total, 1.0)), FLOOR)
            high, low = two_parts(size)
            tail = jnp.where(lane == h, high.astype(F32), tail)
            tail = jnp.where(lane == h + 64, low.astype(F32), tail)
    width = kv_heads * group * HD
    out_ref[:, width : width + HD] = tail.astype(BF)


def states(shape, q, k, v, own, keep):
    vmem = pl.BlockSpec(memory_space=pltpu.VMEM)
    return pl.pallas_call(
        functools.partial(state_kernel, shape),
        out_shape=jax.ShapeDtypeStruct((q.shape[0], q.shape[1] + HD), BF),
        in_specs=[vmem] * 5,
        out_specs=vmem,
        compiler_params=pltpu.CompilerParams(vmem_limit_bytes=16 * 2**20),
        cost_estimate=pl.CostEstimate(flops=4_000_000_000, bytes_accessed=1_500_000, transcendentals=400_000),
    )(q, k, v, own, keep)


def after(values):
    return lax.optimization_barrier(values)


def swap(value, axis):
    return lax.ppermute(value, axis, [(0, 1), (1, 0)])


def local(
    prefill_queries,
    prefill_keys,
    prefill_values,
    segments,
    decode_queries,
    decode_keys,
    decode_values,
    row_request,
    norm_gain,
    head_weight,
    allowed_tiles,
    tokens,
):
    nz, ny, nx = (lax.axis_size(a) for a in CTX)
    nctx = nz * ny * nx
    z, yl, x = (lax.axis_index(a) for a in CTX)
    yh, core = (lax.axis_index(a) for a in TP)
    me = (z * ny + yl) * nx + x
    rows = prefill_queries.shape[0]
    kv_heads = prefill_keys.shape[1] // HD
    width = prefill_queries.shape[1]
    group = width // HD // kv_heads
    half = width // 2
    steps, lines, _ = decode_queries.shape
    model = width * lax.axis_size(TP)

    requests = jnp.arange(REQUESTS, dtype=jnp.int32)
    begins = jnp.sum((segments[None, :] < requests[:, None]).astype(jnp.int32), axis=1)

    own_segment = lax.dynamic_slice_in_dim(segments, me * rows, rows)
    slot = jnp.arange(256, dtype=jnp.int32)[None, None, :] - rows
    key_segment = jnp.pad(own_segment, (0, 256 - rows), constant_values=-1)[None, None, :]
    line = jnp.arange(lines, dtype=jnp.int32)[None, :, None]
    turn = jnp.arange(steps, dtype=jnp.int32)[:, None, None]
    keep = (row_request[None, :, None] == key_segment) | (
        (line == me) & (slot >= 0) & (slot <= turn)
    )
    def mine_and_other(a, w):
        first, second = a[:, :w], a[:, w:]
        return jnp.where(yl == 0, first, second), jnp.where(yl == 0, second, first)

    k_mine, k_other = mine_and_other(prefill_keys, HD)
    v_mine, v_other = mine_and_other(prefill_values, HD)
    kv_mine = jnp.stack([k_mine, v_mine])
    kv_got = swap(jnp.stack([k_other, v_other]), "yl")
    kv_pair = jnp.where(yl == 0, jnp.stack([kv_mine, kv_got]), jnp.stack([kv_got, kv_mine]))
    def mirror(value):
        return lax.ppermute(value, "z", [(i, nz - 1 - i) for i in range(nz)])

    q_mine, q_other = mine_and_other(prefill_queries, half)
    q_far = mirror(q_mine)

    own = jnp.concatenate([decode_keys[:, 0], decode_values[:, 0]], axis=1)
    state = states(
        (steps, lines, kv_heads, group),
        decode_queries.reshape(steps * lines, width),
        prefill_keys,
        prefill_values,
        jnp.pad(own, ((0, 16 - steps), (0, 0))),
        keep.astype(jnp.int32).reshape(steps * lines, 256),
    )
    state = state.reshape(steps, lines, width + HD).transpose(1, 0, 2)
    kv_pair, state, q_far = after((kv_pair, state, q_far))
    kv_all = lax.all_gather(kv_pair, ("z", "x"), axis=0).reshape((nz, nx) + kv_pair.shape)

    met = lax.all_to_all(state, CTX, 0, 0, tiled=True)
    attention = merge(met)
    q_other, attention = after((q_other, attention))
    spread = lax.all_to_all(attention, CTX, 0, 0, tiled=True).reshape(lines * steps, width)

    q_near = swap(q_other, "yl")
    first_rows = jnp.stack([((z * ny + 1 - yl) * nx + x) * rows, ((nz - 1 - z) * ny + yl) * nx * rows + x * rows])
    first_keys = jnp.max(jnp.where(begins[None, :] <= first_rows[:, None], begins[None, :], 0), axis=1)
    plan = jnp.concatenate([first_keys, first_rows, begins])
    spread, q_near, plan = after((spread, q_near, plan))

    widened = spread.astype(F32)
    squares = jnp.sum(widened * widened, axis=1, keepdims=True)
    scaled = (widened * norm_gain).astype(BF)
    partial_logits = dot(scaled, head_weight)
    span = partial_logits.shape[1]

    quarter = span // 4
    high, low = two_parts(squares)
    lane = lax.broadcasted_iota(jnp.int32, (squares.shape[0], 16), 1)
    extra = jnp.where(lane == 0, high, jnp.where(lane == 1, low, jnp.zeros((), BF)))

    def part_of(yh, core):
        return lax.dynamic_slice_in_dim(partial_logits, (core * 2 + yh) * quarter, quarter, 1)

    logits = part_of(yh, core)
    for away in (3, 2, 1):
        sent = part_of(yh ^ (away >> 1), core ^ (away & 1)).astype(BF)
        there = lax.ppermute(
            jnp.concatenate([sent, extra], axis=1), TP, [(i, i ^ away) for i in range(4)]
        )
        logits = logits + there[:, :quarter].astype(F32)
        squares = squares + jnp.sum(there[:, quarter:].astype(F32), axis=1, keepdims=True)
    logits = lax.rsqrt(squares / model + EPS) * logits

    first_id = me * span + core * (span // 2) + yh * quarter
    tiles = first_id // TILE + jnp.arange(quarter // TILE, dtype=jnp.int32)
    allowed = jnp.any(allowed_tiles[..., None] == tiles, axis=2)
    allowed = allowed.transpose(1, 0, 2).reshape(lines * steps, quarter // TILE)
    wanted = tokens.T.reshape(lines * steps, 1) - first_id
    keep_ids = jnp.repeat(allowed, TILE, axis=1)
    masked = jnp.where(keep_ids, logits, FLOOR)
    top = jnp.max(masked, axis=1)
    mass = jnp.sum(jnp.where(keep_ids, jnp.exp(masked - top[:, None]), 0.0), axis=1)
    ids = jnp.arange(quarter, dtype=jnp.int32)
    target = jnp.sum(jnp.where(ids[None, :] == wanted, logits, 0.0), axis=1)

    def joined(top, mass, target, axis):
        peak = jnp.max(top, axis=axis)
        mass = jnp.sum(mass * jnp.exp(top - jnp.expand_dims(peak, axis)), axis=axis)
        return peak, mass, jnp.sum(target, axis=axis)

    stats = jnp.stack([top, mass, target], axis=-1).reshape(lines, steps * 3)
    q_near, q_far, stats = after((q_near, q_far, stats))
    near, far = attend(plan, q_near, q_far, kv_all)
    stats = lax.all_to_all(stats, CTX, 0, 0, tiled=True)
    stats, near, far = after((stats, near, far))
    out_other, out_mine = swap(near, "yl"), mirror(far)
    stats = stats.reshape(nctx, steps, 3)
    stats = jnp.stack(joined(*(stats[..., i] for i in range(3)), 0))
    stats = lax.all_gather(stats, TP, axis=0)
    top, mass, target = joined(*(stats[:, i] for i in range(3)), 0)
    result = target - (top + jnp.log(mass))

    prefill_output = jnp.where(
        yl == 0,
        jnp.concatenate([out_mine, out_other], axis=1),
        jnp.concatenate([out_other, out_mine], axis=1),
    )
    return prefill_output, result[:, None]


def solution(mesh):
    fine = Mesh(mesh.devices.reshape(8, 2, 4, 2, 2), CTX + TP)
    placed = (
        P(CTX, TP),
        P(CTX, TP),
        P(CTX, TP),
        P(),
        P(None, None, TP),
        P(None, CTX, TP),
        P(None, CTX, TP),
        P(),
        P(TP),
        P(TP, CTX),
        P(),
        P(),
    )
    return jax.shard_map(
        local, mesh=fine, in_specs=placed, out_specs=(P(CTX, TP), P(None, CTX)), check_vma=False
    )
```
